128 devices in a mesh: comp: 4 (over x_lo, core), tile: 32 (over z, x_hi, y).
Axes of the slice: x: 4 (x_hi: 2, x_lo: 2; x = x_hi * 2 + x_lo), y: 4, z: 4, core: 2. Of those that a mesh axis runs over, the one named last changes fastest.
Arguments:
- fields: float32 [4, 32, 1966080], P('comp', 'tile'), may hold values from -6 to 6
- atm_mixing: float32 [3, 128, 128], replicated, as said below
- ocean_mixing: float32 [4, 80, 80], replicated, as said below
- sea_mask: int32 [4, 32, 48, 128], P('comp', 'tile'), may hold values 0 or 1
- source_slot: int32 [4, 32, 256], P('comp', 'tile'), may hold values from 0 to 239
- target_tile: int32 [4, 32, 256, 1], P('comp', 'tile'), may hold values from 0 to 31; in each aligned block of 256 rows (0 to 255, 256 to 511, ..., all dimensions but the last counted through in order) at most 16 rows name the same one
- target_slot: int32 [4, 32, 256], P('comp', 'tile'), may hold values from 0 to 239
- remap_blocks: bfloat16 [4, 32, 256, 128, 128], P('comp', 'tile'), may hold values from -0.5 to 0.5
Outputs:
- new_fields: float32 [4, 32, 1966080], P('comp', 'tile')
The draws below stay inside these ranges and needn't reach their ends.
Inputs may be any that keep to these rules, and one draw needn't show every extreme that they name: `target_tile`: among one device's 256 entries no tile is named more than 16 times; in every draw some device names some tile exactly 16 times. `atm_mixing`: each matrix has a diagonal above 0.7 and nonnegative entries whose off-diagonal sum in every row stays below 0.7. `ocean_mixing`: each matrix has a diagonal above 0.7 and nonnegative entries whose off-diagonal sum in every row stays below 0.7.
All inputs are finite; a program needn't handle non-finite values. No bound on the sum of `sea_mask` on one device may be relied on, other than what follows from the above.
Results may differ from the reference program's by a relative error of at most 0.0003.
Values sent between devices are 32-bit elements; how exact they have to be, the bound alone decides.
No kernel may reach another device: no remote copies, remote signals or barrier semaphores. Data moves between devices by JAX's collectives and lax.ppermute only.
A program may use at most 128 MiB of HBM per device.

```python
import math
import jax
import jax.numpy as jnp
import numpy as np
from jax import lax

FA = 3
FO = 4
LA = 128
LO = 80
R = 128
UNIT = 8
P_SIZE = 256
CWO = 48
SLAB = 1966080
CAP = 16
N_COMP = 4
N_TILE = 32


def mixing_matrix(key, fields_count, levels):
    uniform_part = jax.random.uniform(key, (fields_count, levels, levels), jnp.float32)
    places = jnp.arange(levels, dtype=jnp.float32)
    distance = jnp.abs(places[:, None] - places[None, :])
    return 0.7 * jnp.eye(levels, dtype=jnp.float32)[None] + 0.035 * uniform_part * jnp.exp(-distance / 8.0)[None]


def draw_atm_mixing(key, part):
    key = jax.random.fold_in(key, 11)
    return mixing_matrix(key, FA, LA)


def draw_ocean_mixing(key, part):
    key = jax.random.fold_in(key, 23)
    return mixing_matrix(key, FO, LO)


def set_ends(values, rng, low, top_value):
    shape = values.shape
    spot = [jax.random.randint(jax.random.fold_in(rng, axis), (), 0, shape[axis]) for axis in range(len(shape))]
    values = values.at[tuple(spot)].set(low)
    longest = shape.index(max(shape))
    spot[longest] = (spot[longest] + 1) % shape[longest]
    return values.at[tuple(spot)].set(top_value)


def level_of(key, extent, pieces, least, largest):
    level = 1.0
    for dim, parts in pieces:
        draws = jax.random.uniform(jax.random.fold_in(jax.random.fold_in(key, 6), dim), (parts,), jnp.float32, least / len(pieces), largest / len(pieces))
        level = level * jnp.repeat(jnp.exp(draws), extent[dim] // parts).reshape((-1,) + (1,) * (len(extent) - 1 - dim))
    return level


def shared_out(own_key, own, number, rows, count, top, most, slope):
    ranking = jax.random.permutation(own_key, count)
    packed, ordinary = load_shares(count, rows * top, most, slope, True), load_shares(count, rows * top, most, slope, False)
    places = jnp.arange(count)

    def named(lengths, turn):
        used = int((lengths > 0).sum())
        fixed = max(1, used // 4)
        passed = fixed + (places - fixed + turn * (used - fixed)) % max(1, count - fixed)
        return jnp.zeros((count,), jnp.int32).at[ranking[jnp.where(places < fixed, places, passed)]].set(jnp.asarray(lengths, jnp.int32))

    lengths = jnp.where(number % 4 == 0, named(packed, number // 4), named(ordinary, number - number // 4 - 1))
    mixed = jax.random.permutation(jax.random.fold_in(own, 3), count)
    donor, sink = mixed[0:count // 2 * 2:2], mixed[1:count // 2 * 2:2]
    slack = jnp.minimum(lengths[donor] - 1, most - lengths[sink]) // 2
    slack = jnp.where((donor == ranking[0]) | (sink == ranking[0]) | (lengths[sink] == 0), 0, jnp.maximum(slack, 0))
    passed = jax.random.randint(jax.random.fold_in(own, 4), (count // 2,), 0, 1 << 20) % (slack + 1)
    lengths = lengths.at[donor].add(-passed).at[sink].add(passed)
    items = jnp.searchsorted(jnp.cumsum(lengths), jnp.arange(rows * top), side="right").astype(jnp.int32)
    grid = items.reshape(top, rows).T
    grid = grid[jax.random.permutation(jax.random.fold_in(own, 1), rows)]
    turn = jax.random.randint(jax.random.fold_in(own, 2), (rows, 1), 0, top)
    return jnp.take_along_axis(grid, (jnp.arange(top)[None, :] + turn) % top, axis=1)


def load_shares(amount, total, reach, slope, full):
    loads = [(1 << 20) // math.isqrt(grade ** slope) + 1 for grade in range(1, amount + 1)]
    largest = reach if full else min(reach, max(-(-total // amount), total * loads[0] // sum(loads)))
    least = 1 if total - largest >= amount - 1 else 0
    counts, spare = [largest] + [least] * (amount - 1), total - largest - least * (amount - 1)
    while spare > 0:
        movable = [i for i in range(1, amount) if counts[i] < largest] or [i for i in range(1, amount) if counts[i] < reach]
        whole, left = sum([loads[i] for i in movable]), spare
        for i in movable:
            addition = min(reach - counts[i], max(1, left * loads[i] // whole), spare)
            counts[i] = counts[i] + addition
            spare = spare - addition
    return np.array(counts)


def gaussian(rng, shape, width, reach, shards=(), kind=jnp.bfloat16):
    drawn = jax.random.normal(rng, shape, jnp.float32) * width
    if len(shards) > 0:
        drawn = level_of(rng, shape, shards, -0.22, 0.18) * drawn
    return jnp.clip(drawn, min=-reach, max=reach).astype(kind)


def setup_inputs(seed: int = 0) -> dict:
    arg_keys = jax.random.split(jax.random.key(seed), 9)
    fields = gaussian(arg_keys[0], (N_COMP, N_TILE, SLAB), 1.0, 6.0, ((0, 4), (1, 32)), jnp.float32)
    atm_mixing = draw_atm_mixing(jax.random.fold_in(arg_keys[8], 71), 0)
    ocean_mixing = draw_ocean_mixing(jax.random.fold_in(arg_keys[8], 71), 0)
    sea_mask = set_ends((jax.random.randint(arg_keys[3], (N_COMP, N_TILE, CWO, R), 0, 4) < 3).astype(jnp.int32), jax.random.fold_in(arg_keys[3], 1), 0, 1)
    source_slot = set_ends(jax.random.randint(arg_keys[4], (N_COMP, N_TILE, P_SIZE), 0, 30 * UNIT), jax.random.fold_in(arg_keys[4], 1), 0, (30 * UNIT) - 1).astype(jnp.int32)
    target_tile_keys = jax.random.split(jax.random.fold_in(arg_keys[5], 1), N_COMP * N_TILE * P_SIZE // P_SIZE)
    target_tile_turns = jax.random.permutation(jax.random.fold_in(arg_keys[5], 3), N_COMP * N_TILE * P_SIZE // P_SIZE)
    target_tile = jax.vmap(lambda own, number: shared_out(jax.random.fold_in(arg_keys[5], 2), own, number, P_SIZE, N_TILE, 1, CAP, 2))(target_tile_keys, target_tile_turns).reshape((N_COMP, N_TILE, P_SIZE, 1))
    target_slot = set_ends(jax.random.randint(arg_keys[6], (N_COMP, N_TILE, P_SIZE), 0, 30 * UNIT), jax.random.fold_in(arg_keys[6], 1), 0, (30 * UNIT) - 1).astype(jnp.int32)
    remap_blocks = gaussian(arg_keys[7], (N_COMP, N_TILE, P_SIZE, R, R), R ** -0.5, 0.5, ((0, 4), (1, 32)))
    return {"fields": fields, "atm_mixing": atm_mixing, "ocean_mixing": ocean_mixing, "sea_mask": sea_mask, "source_slot": source_slot, "target_tile": target_tile, "target_slot": target_slot, "remap_blocks": remap_blocks}


COUPLE_RATE = 0.1
NU_ATMOS = 0.02
NU_OCEAN = 0.015


def laplace(widened):
    middle = widened[..., 1:-1, :]
    padded = jnp.pad(middle, [(0, 0)] * (middle.ndim - 1) + [(1, 1)])
    return widened[..., 2:, :] + widened[..., :-2, :] + padded[..., 2:] + padded[..., :-2] - 4.0 * middle


def mixing(matrix, column_state):
    return jnp.einsum("flm,fmcr->flcr", matrix, column_state, precision=lax.Precision.HIGHEST)


def dynamics(column_state, matrix, viscosity):
    widened = jnp.concatenate([column_state[:, :, -2:], column_state, column_state[:, :, :2]], axis=2)
    return mixing(matrix, column_state - viscosity * laplace(laplace(widened)))


def contribute(operands):
    surface, sources, weights = operands
    picked = jnp.take(surface, sources % surface.shape[1], axis=1)
    partial_value = jnp.einsum("pij,fpj->pfi", weights.astype(jnp.float32), picked.astype(jnp.float32))
    return partial_value.reshape(partial_value.shape[0], -1)


def reference(fields, atm_mixing, ocean_mixing, sea_mask, source_slot, target_tile, target_slot, remap_blocks):
    atm_cols = 5 * UNIT
    sea_cols = 6 * UNIT
    groups = N_COMP - 1
    atm_dev = fields[:groups].reshape(groups, N_TILE, FA, LA, atm_cols, R)
    sea_dev = fields[groups].reshape(N_TILE, FO, LO, sea_cols, R)
    atm_surface = atm_dev[:, :, :, LA - 1].astype(jnp.bfloat16).reshape(groups * N_TILE, FA, atm_cols, R)
    sea_surface = sea_dev[:, :FA, 0].astype(jnp.bfloat16)
    sources = source_slot.reshape(N_COMP * N_TILE, P_SIZE)
    weights = remap_blocks.reshape(N_COMP * N_TILE, P_SIZE, R, R)
    count_atm = groups * N_TILE
    atm_terms = lax.map(contribute, (atm_surface, sources[:count_atm], weights[:count_atm]))
    sea_terms = lax.map(contribute, (sea_surface, sources[count_atm:], weights[count_atm:]))
    partials = jnp.concatenate([atm_terms, sea_terms], axis=0).reshape(N_COMP * N_TILE * P_SIZE, FA * R)
    targets = target_tile.reshape(N_COMP, N_TILE, P_SIZE)
    is_sea = (jnp.arange(N_COMP) == groups)[:, None, None]
    dest_group = jnp.where(is_sea, (target_slot % (groups * atm_cols)) // atm_cols, groups)
    dest_block = jnp.where(is_sea, target_slot % atm_cols, target_slot % sea_cols)
    row_ids = ((dest_group * N_TILE + targets) * sea_cols + dest_block).reshape(-1).astype(jnp.int32)
    forcing = jax.ops.segment_sum(partials, row_ids, num_segments=N_COMP * N_TILE * sea_cols)
    forcing = forcing.reshape(N_COMP, N_TILE, sea_cols, FA, R)
    sea_flags = sea_mask.astype(jnp.float32)
    results = []
    for group in range(groups):
        column_state = atm_dev[group].transpose(1, 2, 0, 3, 4).reshape(FA, LA, N_TILE * atm_cols, R)
        pushed = forcing[group, :, :atm_cols].transpose(2, 0, 1, 3).reshape(FA, N_TILE * atm_cols, R)
        flags = sea_flags[group, :, :atm_cols].reshape(N_TILE * atm_cols, R)
        column_state = column_state.at[:, LA - 1].add(COUPLE_RATE * pushed * flags)
        for repeat in range(2):
            column_state = dynamics(column_state, atm_mixing, NU_ATMOS)
        column_state = column_state.reshape(FA, LA, N_TILE, atm_cols, R).transpose(2, 0, 1, 3, 4)
        results.append(column_state.reshape(N_TILE, SLAB))
    column_state = sea_dev.transpose(1, 2, 0, 3, 4).reshape(FO, LO, N_TILE * sea_cols, R)
    pushed = forcing[groups].transpose(2, 0, 1, 3).reshape(FA, N_TILE * sea_cols, R)
    flags = sea_flags[groups].reshape(N_TILE * sea_cols, R)
    column_state = column_state.at[:FA, 0].add(COUPLE_RATE * pushed * flags)
    for repeat in range(2):
        column_state = dynamics(column_state, ocean_mixing, NU_OCEAN) * flags
    column_state = column_state.reshape(FO, LO, N_TILE, sea_cols, R).transpose(2, 0, 1, 3, 4)
    results.append(column_state.reshape(N_TILE, SLAB))
    return jnp.stack(results, axis=0)
```

```python
import functools

import jax
import jax.numpy as jnp
from jax import lax
from jax.experimental import pallas as pl
from jax.experimental.pallas import tpu as pltpu
from jax.sharding import PartitionSpec as P

FA = 3
FO = 4
LA = 128
LO = 80
R = 128
CAP = 16

COUPLE_RATE = 0.1
NU_ATMOS = 0.02
NU_OCEAN = 0.015

HALO = 4
CHUNK_ROWS = 56
MIB = 1 << 20


def lane_edges(rows):
    lane = lax.broadcasted_iota(jnp.int32, (rows, R), 1)
    return lane == 0, lane == R - 1


def lap(before, middle, after, edges):
    first, last = edges
    down = jnp.where(first, 0.0, pltpu.roll(middle, 1, 1))
    up = jnp.where(last, 0.0, pltpu.roll(middle, R - 1, 1))
    return (before + after) + (down + up) - 4.0 * middle


def filtered_columns(column, count, nu, mask, edges):
    x, l1, y, l3 = {}, {}, {}, {}
    for k in range(-HALO, count + HALO):
        x[k] = column(k)
        j = k - 1
        if j >= -3:
            l1[j] = lap(x[j - 1], x[j], x[j + 1], edges)
        j = k - 2
        if j >= -2:
            y[j] = x[j] - nu * lap(l1[j - 1], l1[j], l1[j + 1], edges)
            if mask is not None:
                y[j] = y[j] * mask(j)
            x.pop(j - 1, None)
            l1.pop(j - 1, None)
        j = k - 3
        if j >= -1:
            l3[j] = lap(y[j - 1], y[j], y[j + 1], edges)
        j = k - 4
        if j >= 0:
            z = y[j] - nu * lap(l3[j - 1], l3[j], l3[j + 1], edges)
            if mask is not None:
                z = z * mask(j)
            y.pop(j - 1, None)
            l3.pop(j - 1, None)
            yield j, z


def split_two(value):
    high = value.astype(jnp.bfloat16)
    return high, (value - high.astype(jnp.float32)).astype(jnp.bfloat16)


def remap_kernel(per_step, base_ref, idx0_ref, idx1_ref, surf_ref, codes_ref, w_ref, out_ref, lhs_ref):
    step = pl.program_id(0)
    groups = per_step // 4

    @pl.when(step == 0)
    def _():
        out_ref[...] = jnp.zeros_like(out_ref)
        for t in range(codes_ref.shape[0]):
            out_ref[pl.ds(t * CHUNK_ROWS + 3 * CAP, 1), :] = codes_ref[pl.ds(t, 1), :]
        table = surf_ref[...]
        spots = lax.broadcasted_iota(jnp.int32, (idx0_ref.shape[0], table.shape[0]), 1)
        for half, ref in enumerate((idx0_ref, idx1_ref)):
            pick = jnp.where(spots == ref[...], 1.0, 0.0).astype(jnp.bfloat16)
            lhs_ref[:, half * R : (half + 1) * R] = jnp.dot(
                pick, table, preferred_element_type=jnp.float32
            ).astype(jnp.bfloat16)

    for g in range(groups):
        left = w_ref[4 * g : 4 * g + 2].reshape(2 * R, R)
        right = w_ref[4 * g + 2 : 4 * g + 4].reshape(2 * R, R)
        block = jnp.concatenate([left, right], axis=1)
        rows = lhs_ref[pl.ds(pl.multiple_of((step * groups + g) * 16, 16), 16), :]
        res = lax.dot_general(
            rows, block, (((1,), (1,)), ((), ())), preferred_element_type=jnp.float32
        )
        for e in range(4):
            base = base_ref[step * per_step + 4 * g + e]
            half = e % 2
            for f in range(FA):
                out_ref[pl.ds(base + f * CAP, 1), :] = res[
                    f * 4 + e : f * 4 + e + 1, half * R : (half + 1) * R
                ]


def remap(base, idx0, idx1, surf, codes, weights):
    entries = weights.shape[0]
    per_step = 32
    whole = lambda shape: pl.BlockSpec(shape, lambda i, b: (0,) * len(shape))
    n_tile = codes.shape[0]
    out_shape = (n_tile * CHUNK_ROWS, R)
    return pl.pallas_call(
        functools.partial(remap_kernel, per_step),
        out_shape=jax.ShapeDtypeStruct(out_shape, jnp.float32),
        grid_spec=pltpu.PrefetchScalarGridSpec(
            num_scalar_prefetch=1,
            grid=(entries // per_step,),
            in_specs=[
                whole(idx0.shape),
                whole(idx1.shape),
                whole(surf.shape),
                whole(codes.shape),
                pl.BlockSpec((per_step, R, R), lambda i, b: (i, 0, 0)),
            ],
            out_specs=whole(out_shape),
            scratch_shapes=[pltpu.VMEM((entries * 4, 2 * R), jnp.bfloat16)],
        ),
        compiler_params=pltpu.CompilerParams(vmem_limit_bytes=32 * MIB),
        cost_estimate=pl.CostEstimate(
            flops=2 * entries * R * R * 16, bytes_accessed=weights.size * 2, transcendentals=0
        ),
        name="remap",
    )(base, idx0, idx1, surf, codes, weights)


def combine_kernel(rows, recv_ref, out_ref):
    n_tile = recv_ref.shape[0]
    spots = lax.broadcasted_iota(jnp.int32, (rows, R), 0).astype(jnp.float32) + 1.0
    total = [jnp.zeros((rows, R), jnp.float32) for _ in range(FA)]
    for g in range(n_tile // 8):
        code = jnp.sum(recv_ref[g * 8 : (g + 1) * 8, 3 * CAP, :], axis=0, keepdims=True)
        pick = jnp.where(spots == code, 1.0, 0.0).astype(jnp.bfloat16)
        for f in range(FA):
            value = recv_ref[g * 8 : (g + 1) * 8, f * CAP : (f + 1) * CAP, :].reshape(8 * CAP, R)
            high = value.astype(jnp.bfloat16)
            rest = value - high.astype(jnp.float32)
            middle = rest.astype(jnp.bfloat16)
            both = jnp.dot(
                pick,
                jnp.concatenate([high, middle], axis=1),
                preferred_element_type=jnp.float32,
            )
            total[f] = total[f] + (both[:, :R] + both[:, R:])
    per_group = rows // 4
    for f in range(FA):
        for c in range(4):
            out_ref[c, f] = total[f][c * per_group : (c + 1) * per_group]


def combine(recv, sea_cols):
    return pl.pallas_call(
        functools.partial(combine_kernel, 4 * sea_cols),
        out_shape=jax.ShapeDtypeStruct((4, FA, sea_cols, R), jnp.float32),
        compiler_params=pltpu.CompilerParams(vmem_limit_bytes=32 * MIB),
        name="combine",
    )(recv)


def dynamics_part(
    fields, levels, cols, nu, x_ref, left_ref, right_ref, matrix_ref, mask_ref, out_ref, x_vmem, y_vmem, sems
):
    rows_per_field = levels * cols
    copies = []
    for f in range(fields):
        span = pl.ds(f * rows_per_field, rows_per_field)
        copies.append(pltpu.make_async_copy(x_ref.at[span], x_vmem.at[span], sems.at[f]))
        copies[-1].start()
    edges = lane_edges(16)
    for f in range(fields):
        matrix = matrix_ref[f]
        squared = jnp.dot(
            matrix, matrix, precision=lax.Precision.HIGHEST, preferred_element_type=jnp.float32
        )
        high, low = split_two(squared)
        stacked = jnp.concatenate(
            [
                jnp.concatenate([high, high], axis=1),
                jnp.concatenate([low, jnp.zeros_like(low)], axis=1),
            ],
            axis=0,
        )
        copies[f].wait()

        def filter_rows(i, carry, f=f):
            first = f * levels + i * 16

            def column(k):
                if k < 0:
                    return left_ref[pl.ds(first * HALO + k + HALO, 16, stride=HALO), :]
                if k >= cols:
                    return right_ref[pl.ds(first * HALO + k - cols, 16, stride=HALO), :]
                return x_vmem[pl.ds(first * cols + k, 16, stride=cols), :]

            mask = None
            if mask_ref is not None:
                mask = lambda k: jnp.broadcast_to(mask_ref[k + 2 : k + 3, :], (16, R))
            for k, z in filtered_columns(column, cols, nu, mask, edges):
                z_high, z_low = split_two(z)
                spot = pl.multiple_of(i * 16, 16)
                y_vmem[pl.ds(spot, 16), k * R : (k + 1) * R] = z_high
                y_vmem[pl.ds(levels + spot, 16), k * R : (k + 1) * R] = z_low
            return carry

        lax.fori_loop(0, levels // 16, filter_rows, 0)

        for j in range(cols // 2):
            both = jnp.dot(
                stacked,
                y_vmem[: 2 * levels, 2 * j * R : 2 * (j + 1) * R],
                preferred_element_type=jnp.float32,
            )
            mixed = both[:levels] + both[levels:]
            for h in range(2):
                out_ref[pl.ds(f * rows_per_field + 2 * j + h, levels, stride=cols), :] = mixed[
                    :, h * R : (h + 1) * R
                ]


def dynamics_kernel(
    sizes, sea_ref, x_ref, left_ref, right_ref, atm_ref, ocean_ref, mask_ref, out_ref, x_vmem, y_vmem, sems
):
    atm_cols, sea_cols = sizes

    @pl.when(sea_ref[0] == 0)
    def _():
        dynamics_part(
            FA, LA, atm_cols, NU_ATMOS, x_ref, left_ref, right_ref, atm_ref, None, out_ref, x_vmem, y_vmem, sems
        )

    @pl.when(sea_ref[0] != 0)
    def _():
        dynamics_part(
            FO, LO, sea_cols, NU_OCEAN, x_ref, left_ref, right_ref, ocean_ref, mask_ref, out_ref, x_vmem, y_vmem, sems
        )


def dynamics(is_sea, x, left, right, atm_mixing, ocean_mixing, mask, sizes):
    vmem = pl.BlockSpec(memory_space=pltpu.VMEM)
    rows = x.shape[0]
    width = max(sizes) * R
    return pl.pallas_call(
        functools.partial(dynamics_kernel, sizes),
        out_shape=pltpu.VMEM((rows, R), jnp.float32),
        in_specs=[pl.BlockSpec(memory_space=pltpu.SMEM), pl.BlockSpec(memory_space=pl.ANY)] + [vmem] * 5,
        out_specs=vmem,
        scratch_shapes=[
            pltpu.VMEM((rows, R), jnp.float32),
            pltpu.VMEM((2 * LA, width), jnp.bfloat16),
            pltpu.SemaphoreType.DMA((FO,)),
        ],
        compiler_params=pltpu.CompilerParams(vmem_limit_bytes=40 * MIB),
        cost_estimate=pl.CostEstimate(
            flops=8 * rows * R * R, bytes_accessed=24 * rows * R, transcendentals=0
        ),
        name="dynamics",
    )(is_sea, x, left, right, atm_mixing, ocean_mixing, mask)


def filter_forcing(cols, nu, forcing_ref, halo_ref, mask_ref, work_ref, g_ref):
    lo, hi = 8, 8 + cols
    first, last = lane_edges(cols + 16)
    lane_edge = (first, last)
    for f in range(FA):
        work_ref[0 : cols + 16, :] = jnp.zeros((cols + 16, R), jnp.float32)
        work_ref[lo - HALO : lo, :] = halo_ref[0, f]
        work_ref[lo:hi, :] = forcing_ref[f, :cols]
        work_ref[hi : hi + HALO, :] = halo_ref[1, f]
        value = work_ref[0 : cols + 16, :]

        def along(v):
            return lap(pltpu.roll(v, 1, 0), v, pltpu.roll(v, cols + 15, 0), lane_edge)

        value = value - nu * along(along(value))
        if mask_ref is not None:
            value = value * mask_ref[0 : cols + 16, :]
        value = value - nu * along(along(value))
        if mask_ref is not None:
            value = value * mask_ref[0 : cols + 16, :]
        g_ref[f, :cols] = value[lo:hi]


def update_part(cols, column_ref, part_ref, out_ref, g_ref, stage_ref, sems, pieces, levels):
    rows = part_ref.shape[0] // pieces
    per_piece = rows // cols
    for p in range(pieces):
        for q in range(per_piece):
            number = p * per_piece + q
            f = number // levels
            span = pl.ds(number * cols, cols)
            if f < FA:
                stage_ref[span, :] = part_ref[span, :] + column_ref[number] * g_ref[f, :cols]
            else:
                stage_ref[span, :] = part_ref[span, :]
        span = pl.ds(p * rows, rows)
        pltpu.make_async_copy(stage_ref.at[span], out_ref.at[span], sems.at[p]).start()
    for p in range(pieces):
        span = pl.ds(p * rows, rows)
        pltpu.make_async_copy(stage_ref.at[span], out_ref.at[span], sems.at[p]).wait()


def update_kernel(
    sizes, pieces, sea_ref, column_ref, part_ref, forcing_ref, halo_ref, mask_ref, out_ref, work_ref, g_ref, stage_ref, sems
):
    atm_cols, sea_cols = sizes

    @pl.when(sea_ref[0] == 0)
    def _():
        filter_forcing(atm_cols, NU_ATMOS, forcing_ref, halo_ref, None, work_ref, g_ref)
        update_part(atm_cols, column_ref, part_ref, out_ref, g_ref, stage_ref, sems, pieces, LA)

    @pl.when(sea_ref[0] != 0)
    def _():
        filter_forcing(sea_cols, NU_OCEAN, forcing_ref, halo_ref, mask_ref, work_ref, g_ref)
        update_part(sea_cols, column_ref, part_ref, out_ref, g_ref, stage_ref, sems, pieces, LO)


def update(is_sea, column, part, forcing, halo, mask, sizes):
    vmem = pl.BlockSpec(memory_space=pltpu.VMEM)
    smem = pl.BlockSpec(memory_space=pltpu.SMEM)
    rows = part.shape[0]
    pieces = 8
    return pl.pallas_call(
        functools.partial(update_kernel, sizes, pieces),
        out_shape=jax.ShapeDtypeStruct((rows, R), jnp.float32),
        in_specs=[smem, smem, vmem, vmem, vmem, vmem],
        out_specs=pl.BlockSpec(memory_space=pl.ANY),
        scratch_shapes=[
            pltpu.VMEM((max(sizes) + 16, R), jnp.float32),
            pltpu.VMEM((FA, max(sizes), R), jnp.float32),
            pltpu.VMEM((rows, R), jnp.float32),
            pltpu.SemaphoreType.DMA((pieces,)),
        ],
        compiler_params=pltpu.CompilerParams(vmem_limit_bytes=40 * MIB),
        cost_estimate=pl.CostEstimate(
            flops=2 * rows * R, bytes_accessed=8 * rows * R, transcendentals=0
        ),
        name="update",
    )(is_sea, column, part, forcing, halo, mask)


def local(
    fields, atm_mixing, ocean_mixing, sea_mask, source_slot, target_tile, target_slot, remap_blocks
):
    n_comp = lax.axis_size("comp")
    n_tile = lax.axis_size("tile")
    groups = n_comp - 1
    is_sea = lax.axis_index("comp") == groups
    sea_cols = sea_mask.shape[2]
    atm_cols = sea_cols * 5 // 6
    sizes = (atm_cols, sea_cols)
    sea_flag = is_sea.astype(jnp.int32).reshape(1)
    mask = sea_mask[0, 0].astype(jnp.float32)
    state = fields[0, 0]
    sources = source_slot[0, 0]
    tiles = target_tile[0, 0, :, 0]
    codes = target_slot[0, 0]
    weights = remap_blocks[0, 0]
    entries = sources.shape[0]
    forward = [(i, (i + 1) % n_tile) for i in range(n_tile)]
    backward = [(b, a) for a, b in forward]

    def atm_edges(values):
        split = values.reshape(FA * LA, atm_cols // HALO, HALO, R)
        return split[:, 0], split[:, -1]

    def sea_edges(values):
        split = values.reshape(FO * LO, sea_cols // HALO, HALO, R)
        spare = FA * LA - FO * LO
        cut = mask.reshape(sea_cols // HALO, HALO, R)
        fill = lambda edge, own: jnp.concatenate(
            [edge, own[None], jnp.zeros((spare - 1, HALO, R), jnp.float32)], axis=0
        )
        return fill(split[:, 0], cut[0]), fill(split[:, -1], cut[-1])

    low_edge, high_edge = lax.cond(is_sea, sea_edges, atm_edges, state)
    left = lax.ppermute(high_edge, "tile", forward)
    right = lax.ppermute(low_edge, "tile", backward)

    def atm_surface(values):
        top = values.reshape(FA, LA, atm_cols, R)[:, LA - 1]
        return jnp.pad(top, ((0, 0), (0, sea_cols - atm_cols), (0, 0))).astype(jnp.bfloat16)

    def sea_surface(values):
        return values.reshape(FO, LO, sea_cols, R)[:FA, 0].astype(jnp.bfloat16)

    surface = lax.cond(is_sea, sea_surface, atm_surface, state).reshape(FA * sea_cols, R)
    source = jnp.where(is_sea, sources % sea_cols, sources % atm_cols)
    order = jnp.arange(entries)
    same = (tiles[:, None] == tiles[None, :]) & (order[None, :] < order[:, None])
    rank = jnp.sum(same.astype(jnp.int32), axis=1)
    base = tiles * CHUNK_ROWS + rank
    row = jnp.arange(16)
    pick_row = source.reshape(entries // 4, 1, 4) + (jnp.arange(4) * sea_cols)[None, :, None]
    pick_row = pick_row.reshape(entries // 4, 16)
    in_use = row < 4 * FA
    idx0 = jnp.where(in_use & (row % 4 < 2), pick_row, -1).reshape(entries * 4, 1)
    idx1 = jnp.where(in_use & (row % 4 >= 2), pick_row, -1).reshape(entries * 4, 1)
    dest_group = jnp.where(is_sea, codes % (groups * atm_cols) // atm_cols, groups)
    dest_block = jnp.where(is_sea, codes % atm_cols, codes % sea_cols)
    dest_row = (dest_group * sea_cols + dest_block + 1).astype(jnp.float32)
    slots = jnp.arange(n_tile * CAP)
    slot_code = jnp.sum(
        jnp.where(slots[:, None] == (tiles * CAP + rank)[None, :], dest_row[None, :], 0.0), axis=1
    ).reshape(n_tile, 1, CAP)
    per_row = R // CAP
    own_part = (jnp.arange(per_row) == lax.axis_index("tile") % per_row).astype(jnp.float32)
    code_rows = (slot_code * own_part[None, :, None]).reshape(n_tile, R)
    sent = remap(base, idx0, idx1, surface, code_rows, weights)
    received = lax.all_to_all(
        sent.reshape(n_tile, CHUNK_ROWS, R), "tile", split_axis=0, concat_axis=0, tiled=True
    )

    flat_left = left.reshape(FA * LA * HALO, R)
    flat_right = right.reshape(FA * LA * HALO, R)
    mask_left, mask_right = left[FO * LO], right[FO * LO]
    wide_mask = jnp.concatenate([mask_left[2:], mask, mask_right[:2]], axis=0)
    part = dynamics(
        sea_flag,
        state.reshape(-1, R),
        flat_left,
        flat_right,
        atm_mixing,
        ocean_mixing,
        wide_mask,
        sizes,
    )

    shares = lax.all_to_all(combine(received, sea_cols), "comp", split_axis=0, concat_axis=0, tiled=True)
    pushed = COUPLE_RATE * jnp.sum(shares, axis=0) * mask
    low_part = pushed[:, :HALO]
    high_part = jnp.where(is_sea, pushed[:, sea_cols - HALO :], pushed[:, atm_cols - HALO : atm_cols])
    halo = jnp.stack(
        [lax.ppermute(high_part, "tile", forward), lax.ppermute(low_part, "tile", backward)]
    )
    atm_column = jnp.einsum(
        "flm,fm->fl", atm_mixing, atm_mixing[:, :, LA - 1], precision=lax.Precision.HIGHEST
    ).reshape(-1)
    ocean_column = jnp.einsum(
        "flm,fm->fl", ocean_mixing, ocean_mixing[:, :, 0], precision=lax.Precision.HIGHEST
    ).reshape(-1)
    ocean_column = jnp.pad(ocean_column, (0, FA * LA - FO * LO))
    column = jnp.where(is_sea, ocean_column, atm_column)
    work_mask = jnp.concatenate(
        [jnp.zeros((4, R), jnp.float32), mask_left, mask, mask_right, jnp.zeros((4, R), jnp.float32)], axis=0
    )
    done = update(sea_flag, column, part, pushed, halo, work_mask, sizes)
    return done.reshape(1, 1, -1)


def solution(mesh):
    in_specs = (
        P("comp", "tile", None),
        P(),
        P(),
        P("comp", "tile", None, None),
        P("comp", "tile", None),
        P("comp", "tile", None, None),
        P("comp", "tile", None),
        P("comp", "tile", None, None, None),
    )
    out_specs = P("comp", "tile", None)
    return jax.shard_map(local, mesh=mesh, in_specs=in_specs, out_specs=out_specs, check_vma=False)
```

```python
import functools

import jax
import jax.numpy as jnp
import numpy as np
from jax import lax
from jax.experimental import pallas as pl
from jax.experimental.pallas import tpu as pltpu
from jax.sharding import PartitionSpec as P

FA = 3
FO = 4
LA = 128
LO = 80
R = 128
CAP = 16

COUPLE_RATE = 0.1
NU_ATMOS = 0.02
NU_OCEAN = 0.015

HALO = 4
CHUNK_ROWS = 56
MIB = 1 << 20


def split_two(value):
    high = value.astype(jnp.bfloat16)
    return high, (value - high.astype(jnp.float32)).astype(jnp.bfloat16)


def row_operator():
    u = np.eye(R, k=1) + np.eye(R, k=-1) - 4.0 * np.eye(R)
    both = np.concatenate([2.0 * u, u @ u + 2.0 * np.eye(R)], axis=1)
    return jnp.asarray(np.concatenate([both, both], axis=0), jnp.bfloat16)


def apply_filter(value, column_sums, row_parts, nu):
    return value - nu * (column_sums + row_parts)


def filter_planes(column, spans, nu, mask, operator, lhs_ref, emit):
    rows = 16
    places = {}
    for first, last in spans:
        for k in range(first - 1, last + 1):
            spot = places[first, k] = len(places) * rows
            high, low = split_two(column(k))
            lhs_ref[spot : spot + rows, :R] = high
            lhs_ref[spot : spot + rows, R:] = low
    both = jnp.dot(lhs_ref[: len(places) * rows], operator, preferred_element_type=jnp.float32)

    def part(place, half):
        spot = places[place]
        return both[spot : spot + rows, half * R : (half + 1) * R]

    for first, last in spans:
        for k in range(first, last):
            column_sums = column(k - 2) + column(k + 2)
            row_parts = (part((first, k - 1), 0) + part((first, k + 1), 0)) + part((first, k), 1)
            plane = apply_filter(column(k), column_sums, row_parts, nu)
            if mask is not None:
                plane = plane * mask(k)
            emit(k, plane)


def stacked_square(matrix):
    squared = jnp.dot(
        matrix, matrix, precision=lax.Precision.HIGHEST, preferred_element_type=jnp.float32
    )
    high, low = split_two(squared)
    return jnp.concatenate(
        [
            jnp.concatenate([high, high], axis=1),
            jnp.concatenate([low, jnp.zeros_like(low)], axis=1),
        ],
        axis=0,
    )


def surface_copies(sizes, sea, x_ref, surf_ref, sems):
    atm_cols, sea_cols = sizes
    if sea:
        cols, starts = sea_cols, [f * LO * sea_cols for f in range(FA)]
    else:
        cols, starts = atm_cols, [(f * LA + LA - 1) * atm_cols for f in range(FA)]
    return [
        pltpu.make_async_copy(
            x_ref.at[pl.ds(start, cols)], surf_ref.at[pl.ds(f * sea_cols, cols)], sems.at[f]
        )
        for f, start in enumerate(starts)
    ]


def small_mod(value, modulus, limit):
    for step in range(modulus, limit, modulus):
        value = jnp.where(value >= modulus, value - modulus, value)
    return value


def as_column(row):
    n = row.shape[1]
    diagonal = lax.broadcasted_iota(jnp.int32, (n, n), 0) == lax.broadcasted_iota(jnp.int32, (n, n), 1)
    return jnp.sum(jnp.where(diagonal, row, 0.0), axis=1, keepdims=True)


def ones_where(condition):
    return jnp.where(condition, 1.0, 0.0).astype(jnp.bfloat16)


def remap_kernel(
    sizes, n_tile, chunks, place_ref, source_ref, tile_ref, slot_ref, x_ref, w_ref, out_ref, w_vmem, surf_ref, pick_ref, part_ref, w_sems, x_sems
):
    atm_cols, sea_cols = sizes
    entries = source_ref.shape[1]
    quarter = entries // 4
    per_chunk = quarter // chunks
    code_limit = 5 * sea_cols
    copies = [
        pltpu.make_async_copy(
            w_ref.at[:, pl.ds(n * per_chunk, per_chunk)], w_vmem.at[:, pl.ds(n * per_chunk, per_chunk)], w_sems.at[n]
        )
        for n in range(chunks)
    ]
    is_sea = place_ref[0] != 0
    for sea in (False, True):

        @pl.when(is_sea == sea)
        def _(sea=sea):
            for copy in surface_copies(sizes, sea, x_ref, surf_ref, x_sems):
                copy.start()

    for copy in copies:
        copy.start()

    tile = tile_ref[...].astype(jnp.float32)
    tile_column = as_column(tile)
    earlier = lax.broadcasted_iota(jnp.int32, (entries, entries), 0) < lax.broadcasted_iota(
        jnp.int32, (entries, entries), 1
    )
    rank = jnp.sum(jnp.where((tile_column == tile) & earlier, 1.0, 0.0), axis=0, keepdims=True)
    code = slot_ref[...]
    for_atm = small_mod(code, 3 * atm_cols, code_limit)
    for_atm_block = small_mod(for_atm, atm_cols, 3 * atm_cols)
    for_atm_group = jnp.where(for_atm >= atm_cols, 1, 0) + jnp.where(for_atm >= 2 * atm_cols, 1, 0)
    for_sea = 3 * sea_cols + small_mod(code, sea_cols, code_limit)
    dest = jnp.where(is_sea, for_atm_group * sea_cols + for_atm_block, for_sea)
    dest = (dest + 1).astype(jnp.float32)
    lane = rank + (CAP * lax.rem(place_ref[1], R // CAP)).astype(jnp.float32)
    spots = lax.broadcasted_iota(jnp.int32, (R, entries), 0).astype(jnp.float32)
    marks = jnp.where(spots == lane, dest, 0.0).astype(jnp.bfloat16)
    tiles = lax.broadcasted_iota(jnp.int32, (n_tile, entries), 0).astype(jnp.float32)
    codes = lax.dot_general(
        ones_where(tiles == tile), marks, (((1,), (1,)), ((), ())), preferred_element_type=jnp.float32
    )
    tail = CHUNK_ROWS - FA * CAP
    for t in range(n_tile):
        out_ref[t, FA * CAP :, :] = jnp.concatenate(
            [codes[t : t + 1], jnp.zeros((tail - 1, R), jnp.float32)], axis=0
        )

    source = source_ref[...]
    source = jnp.where(
        is_sea, small_mod(source, sea_cols, code_limit), small_mod(source, atm_cols, code_limit)
    )
    source_column = as_column(source.astype(jnp.float32))
    columns = lax.broadcasted_iota(jnp.int32, (entries, sea_cols), 1).astype(jnp.float32)
    chooser = ones_where(columns == source_column)
    for sea in (False, True):

        @pl.when(is_sea == sea)
        def _(sea=sea):
            for copy in surface_copies(sizes, sea, x_ref, surf_ref, x_sems):
                copy.wait()
            if not sea:
                for f in range(FA):
                    surf_ref[f * sea_cols + atm_cols : (f + 1) * sea_cols, :] = jnp.zeros(
                        (sea_cols - atm_cols, R), jnp.float32
                    )

    for f in range(FA):
        surface = surf_ref[f * sea_cols : (f + 1) * sea_cols, :].astype(jnp.bfloat16)
        pick_ref[f * entries : (f + 1) * entries, :] = jnp.dot(
            chooser, surface, preferred_element_type=jnp.float32
        )
    pick_ref[FA * entries :, :] = jnp.zeros((entries, R), jnp.float32)

    member = lax.rem(lax.broadcasted_iota(jnp.int32, (16, R), 0), 4)
    for n in range(chunks):
        copies[n].wait()
        for g in range(n * per_chunk, (n + 1) * per_chunk):
            picked = pick_ref[pl.ds(g, 16, stride=quarter), :]
            rows = jnp.concatenate(
                [jnp.where(member < 2, picked, 0.0), jnp.where(member >= 2, picked, 0.0)], axis=1
            ).astype(jnp.bfloat16)
            block = jnp.concatenate(
                [
                    jnp.concatenate([w_vmem[0, g], w_vmem[2, g]], axis=1),
                    jnp.concatenate([w_vmem[1, g], w_vmem[3, g]], axis=1),
                ],
                axis=0,
            )
            res = lax.dot_general(
                rows, block, (((1,), (1,)), ((), ())), preferred_element_type=jnp.float32
            )
            part_ref[pl.ds(g, 16, stride=quarter), :] = jnp.where(member % 2 == 0, res[:, :R], res[:, R:])

    slot = tile * CAP + rank
    slots = lax.broadcasted_iota(jnp.int32, (n_tile * CAP, entries), 0).astype(jnp.float32)
    placer = ones_where(slots == slot)
    for f in range(FA):
        high, low = split_two(part_ref[f * entries : (f + 1) * entries, :])
        both = jnp.dot(placer, jnp.concatenate([high, low], axis=1), preferred_element_type=jnp.float32)
        placed = both[:, :R] + both[:, R:]
        for t in range(n_tile):
            out_ref[t, f * CAP : (f + 1) * CAP, :] = placed[t * CAP : (t + 1) * CAP]


def remap(place, source, tile, slot, x, weights, n_tile, sizes):
    entries = weights.shape[0]
    chunks = 8
    vmem = pl.BlockSpec(memory_space=pltpu.VMEM)
    anywhere = pl.BlockSpec(memory_space=pl.ANY)
    return pl.pallas_call(
        functools.partial(remap_kernel, sizes, n_tile, chunks),
        out_shape=jax.ShapeDtypeStruct((n_tile, CHUNK_ROWS, R), jnp.float32),
        in_specs=[pl.BlockSpec(memory_space=pltpu.SMEM), vmem, vmem, vmem, anywhere, anywhere],
        out_specs=vmem,
        scratch_shapes=[
            pltpu.VMEM((4, entries // 4, R, R), jnp.bfloat16),
            pltpu.VMEM((FA * sizes[1], R), jnp.float32),
            pltpu.VMEM((4 * entries, R), jnp.float32),
            pltpu.VMEM((4 * entries, R), jnp.float32),
            pltpu.SemaphoreType.DMA((chunks,)),
            pltpu.SemaphoreType.DMA((FA,)),
        ],
        compiler_params=pltpu.CompilerParams(vmem_limit_bytes=56 * MIB),
        cost_estimate=pl.CostEstimate(
            flops=2 * entries * R * R * 16, bytes_accessed=weights.size * 2, transcendentals=0
        ),
        name="remap",
    )(place, source, tile, slot, x, weights.reshape(4, entries // 4, R, R))


def combine_kernel(rows, recv_ref, out_ref):
    n_tile = recv_ref.shape[0]
    spots = lax.broadcasted_iota(jnp.int32, (rows, R), 0).astype(jnp.float32) + 1.0
    total = [jnp.zeros((rows, R), jnp.float32) for _ in range(FA)]
    for g in range(n_tile // 8):
        code = jnp.sum(recv_ref[g * 8 : (g + 1) * 8, 3 * CAP, :], axis=0, keepdims=True)
        pick = jnp.where(spots == code, 1.0, 0.0).astype(jnp.bfloat16)
        for f in range(FA):
            value = recv_ref[g * 8 : (g + 1) * 8, f * CAP : (f + 1) * CAP, :].reshape(8 * CAP, R)
            high = value.astype(jnp.bfloat16)
            rest = value - high.astype(jnp.float32)
            middle = rest.astype(jnp.bfloat16)
            both = jnp.dot(
                pick,
                jnp.concatenate([high, middle], axis=1),
                preferred_element_type=jnp.float32,
            )
            total[f] = total[f] + (both[:, :R] + both[:, R:])
    per_group = rows // 4
    for f in range(FA):
        for c in range(4):
            out_ref[c, f] = total[f][c * per_group : (c + 1) * per_group]


def combine(recv, sea_cols):
    return pl.pallas_call(
        functools.partial(combine_kernel, 4 * sea_cols),
        out_shape=jax.ShapeDtypeStruct((4, FA, sea_cols, R), jnp.float32),
        compiler_params=pltpu.CompilerParams(vmem_limit_bytes=32 * MIB),
        name="combine",
    )(recv)


def filtered_twice(levels, cols, inner, outer, nu, column, mask, operator, lhs_ref, mid_ref, store):
    order = {k: n for n, k in enumerate(k for first, last in inner for k in range(first, last))}

    def middle(k):
        return mid_ref[order[k] * 16 : (order[k] + 1) * 16, :]

    def keep(k, plane):
        mid_ref[order[k] * 16 : (order[k] + 1) * 16, :] = plane

    filter_planes(column, inner, nu, mask, operator, lhs_ref.at[0], keep)
    filter_planes(middle, outer, nu, mask, operator, lhs_ref.at[1], store)


def mixed_planes(stacked, y_vmem, levels, pair):
    both = jnp.dot(
        stacked,
        y_vmem[: 2 * levels, 2 * pair * R : 2 * (pair + 1) * R],
        preferred_element_type=jnp.float32,
    )
    return both[:levels] + both[levels:]


def plane_store(y_vmem, levels, i, first_plane):
    spot = pl.multiple_of(i * 16, 16)

    def store(k, plane):
        high, low = split_two(plane)
        lanes = slice((k - first_plane) * R, (k - first_plane + 1) * R)
        y_vmem[pl.ds(spot, 16), lanes] = high
        y_vmem[pl.ds(levels + spot, 16), lanes] = low

    return store


def inner_part(
    fields, levels, cols, nu, x_ref, matrix_ref, mask_ref, op_ref, out_ref, x_vmem, y_vmem, lhs_ref, mid_ref, out_vmem, in_sems, out_sems
):
    rows_per_field = levels * cols
    spans = [pl.ds(f * rows_per_field, rows_per_field) for f in range(fields)]
    reads = [pltpu.make_async_copy(x_ref.at[s], x_vmem.at[s], in_sems.at[f]) for f, s in enumerate(spans)]
    writes = [pltpu.make_async_copy(out_vmem.at[s], out_ref.at[s], out_sems.at[f]) for f, s in enumerate(spans)]
    for read in reads:
        read.start()
    mask = None
    if mask_ref is not None:
        mask = lambda k: jnp.broadcast_to(mask_ref[k : k + 1, :], (16, R))
    for f in range(fields):
        stacked = stacked_square(matrix_ref[f])
        reads[f].wait()

        def filter_rows(i, carry, f=f):
            first = f * levels + i * 16
            column = lambda k: x_vmem[pl.ds(first * cols + k, 16, stride=cols), :]
            filtered_twice(
                levels, cols, [(2, cols - 2)], [(HALO, cols - HALO)], nu, column, mask, op_ref[...], lhs_ref, mid_ref,
                plane_store(y_vmem, levels, i, HALO),
            )
            return carry

        lax.fori_loop(0, levels // 16, filter_rows, 0)

        for pair in range((cols - 2 * HALO) // 2):
            mixed = mixed_planes(stacked, y_vmem, levels, pair)
            for h in range(2):
                k = HALO + 2 * pair + h
                out_vmem[pl.ds(f * rows_per_field + k, levels, stride=cols), :] = mixed[:, h * R : (h + 1) * R]
        writes[f].start()
    for write in writes:
        write.wait()


def inner_kernel(sizes, sea_ref, x_ref, atm_ref, ocean_ref, mask_ref, op_ref, out_ref, *scratch):
    atm_cols, sea_cols = sizes

    @pl.when(sea_ref[0] == 0)
    def _():
        inner_part(FA, LA, atm_cols, NU_ATMOS, x_ref, atm_ref, None, op_ref, out_ref, *scratch)

    @pl.when(sea_ref[0] != 0)
    def _():
        inner_part(FO, LO, sea_cols, NU_OCEAN, x_ref, ocean_ref, mask_ref, op_ref, out_ref, *scratch)


def inner_dynamics(is_sea, x, atm_mixing, ocean_mixing, mask, sizes):
    vmem = pl.BlockSpec(memory_space=pltpu.VMEM)
    anywhere = pl.BlockSpec(memory_space=pl.ANY)
    rows = x.shape[0]
    widest = max(sizes)
    return pl.pallas_call(
        functools.partial(inner_kernel, sizes),
        out_shape=jax.ShapeDtypeStruct((rows, R), jnp.float32),
        in_specs=[pl.BlockSpec(memory_space=pltpu.SMEM), anywhere] + [vmem] * 4,
        out_specs=anywhere,
        scratch_shapes=[
            pltpu.VMEM((rows, R), jnp.float32),
            pltpu.VMEM((2 * LA, (widest - 2 * HALO) * R), jnp.bfloat16),
            pltpu.VMEM((2, widest * 16, 2 * R), jnp.bfloat16),
            pltpu.VMEM((widest * 16, R), jnp.float32),
            pltpu.VMEM((rows, R), jnp.float32),
            pltpu.SemaphoreType.DMA((FO,)),
            pltpu.SemaphoreType.DMA((FO,)),
        ],
        compiler_params=pltpu.CompilerParams(vmem_limit_bytes=56 * MIB),
        cost_estimate=pl.CostEstimate(
            flops=2 * rows * R * R, bytes_accessed=2 * rows * R, transcendentals=0
        ),
        name="inner_dynamics",
    )(is_sea, x, atm_mixing, ocean_mixing, mask, row_operator())


def rim_part(
    fields, levels, cols, nu, x_ref, left_ref, right_ref, matrix_ref, mask_ref, op_ref, out_ref, low_vmem, high_vmem, y_vmem, lhs_ref, mid_ref, sems
):
    count, count_all = fields * levels, low_vmem.shape[0]
    copies = [
        pltpu.make_async_copy(x_ref.at[:, pl.ds(start, 8), :], vmem.at[pl.ds(0, count)], sems.at[n])
        for n, (start, vmem) in enumerate(((0, low_vmem), (cols - 8, high_vmem)))
    ]
    for copy in copies:
        copy.start()
    mask = None
    if mask_ref is not None:
        mask = lambda k: jnp.broadcast_to(mask_ref[k + HALO : k + HALO + 1, :], (16, R))
    for copy in copies:
        copy.wait()
    low_vmem, high_vmem = (v.reshape(count_all * 8, R) for v in (low_vmem, high_vmem))
    for f in range(fields):
        stacked = stacked_square(matrix_ref[f])

        def filter_rows(i, carry, f=f):
            first = pl.multiple_of(f * levels + i * 16, 16)

            def column(k):
                if k < 0:
                    return left_ref[pl.ds(first * HALO + k + HALO, 16, stride=HALO), :]
                if k < 8:
                    return low_vmem[pl.ds(first * 8 + k, 16, stride=8), :]
                if k < cols:
                    return high_vmem[pl.ds(first * 8 + k - (cols - 8), 16, stride=8), :]
                return right_ref[pl.ds(first * HALO + k - cols, 16, stride=HALO), :]

            store = plane_store(y_vmem, levels, i, 0)
            filtered_twice(
                levels, cols, [(-2, 6), (cols - 6, cols + 2)], [(0, HALO), (cols - HALO, cols)], nu, column, mask,
                op_ref[...], lhs_ref, mid_ref, lambda k, plane: store(k if k < HALO else k - cols + 2 * HALO, plane),
            )
            return carry

        lax.fori_loop(0, levels // 16, filter_rows, 0)
        for pair in range(HALO):
            mixed = mixed_planes(stacked, y_vmem, levels, pair)
            for h in range(2):
                out_ref[pl.ds(f * levels * 8 + 2 * pair + h, levels, stride=8), :] = mixed[:, h * R : (h + 1) * R]


def rim_kernel(
    sizes, sea_ref, x_atm_ref, x_sea_ref, left_ref, right_ref, atm_ref, ocean_ref, mask_ref, op_ref, out_ref, *scratch
):
    atm_cols, sea_cols = sizes

    @pl.when(sea_ref[0] == 0)
    def _():
        rim_part(
            FA, LA, atm_cols, NU_ATMOS, x_atm_ref, left_ref, right_ref, atm_ref, None, op_ref, out_ref, *scratch
        )

    @pl.when(sea_ref[0] != 0)
    def _():
        rim_part(
            FO, LO, sea_cols, NU_OCEAN, x_sea_ref, left_ref, right_ref, ocean_ref, mask_ref, op_ref, out_ref, *scratch
        )


def rim_dynamics(is_sea, x_atm, x_sea, left, right, atm_mixing, ocean_mixing, mask, sizes):
    vmem = pl.BlockSpec(memory_space=pltpu.VMEM)
    anywhere = pl.BlockSpec(memory_space=pl.ANY)
    count = x_atm.shape[0]
    return pl.pallas_call(
        functools.partial(rim_kernel, sizes),
        out_shape=jax.ShapeDtypeStruct((count * 8, R), jnp.float32),
        in_specs=[pl.BlockSpec(memory_space=pltpu.SMEM), anywhere, anywhere] + [vmem] * 6,
        out_specs=vmem,
        scratch_shapes=[
            pltpu.VMEM((count, 8, R), jnp.float32),
            pltpu.VMEM((count, 8, R), jnp.float32),
            pltpu.VMEM((2 * LA, 8 * R), jnp.bfloat16),
            pltpu.VMEM((2, 20 * 16, 2 * R), jnp.bfloat16),
            pltpu.VMEM((16 * 16, R), jnp.float32),
            pltpu.SemaphoreType.DMA((2,)),
        ],
        compiler_params=pltpu.CompilerParams(vmem_limit_bytes=16 * MIB),
        cost_estimate=pl.CostEstimate(
            flops=20 * count * 40 * R * R, bytes_accessed=count * 24 * R * 4, transcendentals=0
        ),
        name="rim_dynamics",
    )(is_sea, x_atm, x_sea, left, right, atm_mixing, ocean_mixing, mask, row_operator())


def lane_edges(rows):
    lane = lax.broadcasted_iota(jnp.int32, (rows, R), 1)
    return lane == 0, lane == R - 1


def lap(before, middle, after, edges):
    first, last = edges
    down = jnp.where(first, 0.0, pltpu.roll(middle, 1, 1))
    up = jnp.where(last, 0.0, pltpu.roll(middle, R - 1, 1))
    return (before + after) + (down + up) - 4.0 * middle


def filter_forcing(cols, nu, forcing_ref, halo_ref, mask_ref, work_ref, g_ref):
    lo, hi = 8, 8 + cols
    first, last = lane_edges(cols + 16)
    lane_edge = (first, last)
    for f in range(FA):
        work_ref[0 : cols + 16, :] = jnp.zeros((cols + 16, R), jnp.float32)
        work_ref[lo - HALO : lo, :] = halo_ref[0, f]
        work_ref[lo:hi, :] = forcing_ref[f, :cols]
        work_ref[hi : hi + HALO, :] = halo_ref[1, f]
        value = work_ref[0 : cols + 16, :]

        def along(v):
            return lap(pltpu.roll(v, 1, 0), v, pltpu.roll(v, cols + 15, 0), lane_edge)

        value = value - nu * along(along(value))
        if mask_ref is not None:
            value = value * mask_ref[0 : cols + 16, :]
        value = value - nu * along(along(value))
        if mask_ref is not None:
            value = value * mask_ref[0 : cols + 16, :]
        g_ref[f, :cols] = value[lo:hi]


def update_part(cols, levels, pieces, nu, column_ref, part_ref, rim_ref, forcing_ref, halo_ref, mask_ref, out_ref, work_ref, g_ref, stage_ref, in_sems, out_sems):
    rows = part_ref.shape[0] // pieces
    spans = [pl.ds(p * rows, rows) for p in range(pieces)]
    reads = [pltpu.make_async_copy(part_ref.at[s], stage_ref.at[s], in_sems.at[p]) for p, s in enumerate(spans)]
    writes = [pltpu.make_async_copy(stage_ref.at[s], out_ref.at[s], out_sems.at[p]) for p, s in enumerate(spans)]
    for read in reads:
        read.start()
    filter_forcing(cols, nu, forcing_ref, halo_ref, mask_ref, work_ref, g_ref)
    upper = lax.broadcasted_iota(jnp.int32, (8, R), 0) < HALO
    for p in range(pieces):
        reads[p].wait()
        for number in range(p * rows // cols, (p + 1) * rows // cols):
            f = number // levels
            rim = rim_ref[number * 8 : (number + 1) * 8, :]
            for v in range(cols // 8):
                span = slice(number * cols + v * 8, number * cols + v * 8 + 8)
                if f >= FA and 0 < v < cols // 8 - 1:
                    continue
                value = stage_ref[span, :]
                if v == 0:
                    value = jnp.where(upper, rim, value)
                if v == cols // 8 - 1:
                    value = jnp.where(upper, value, rim)
                if f < FA:
                    value = value + column_ref[number] * g_ref[f, v * 8 : v * 8 + 8, :]
                stage_ref[span, :] = value
        writes[p].start()
    for write in writes:
        write.wait()


def update_kernel(
    sizes, pieces, sea_ref, column_ref, part_ref, rim_ref, forcing_ref, halo_ref, mask_ref, *rest
):
    atm_cols, sea_cols = sizes

    @pl.when(sea_ref[0] == 0)
    def _():
        update_part(
            atm_cols, LA, pieces, NU_ATMOS, column_ref, part_ref, rim_ref, forcing_ref, halo_ref, None, *rest
        )

    @pl.when(sea_ref[0] != 0)
    def _():
        update_part(
            sea_cols, LO, pieces, NU_OCEAN, column_ref, part_ref, rim_ref, forcing_ref, halo_ref, mask_ref, *rest
        )


def update(is_sea, column, part, rim, forcing, halo, mask, sizes):
    vmem = pl.BlockSpec(memory_space=pltpu.VMEM)
    smem = pl.BlockSpec(memory_space=pltpu.SMEM)
    anywhere = pl.BlockSpec(memory_space=pl.ANY)
    rows = part.shape[0]
    pieces = 8
    return pl.pallas_call(
        functools.partial(update_kernel, sizes, pieces),
        out_shape=jax.ShapeDtypeStruct((rows, R), jnp.float32),
        in_specs=[smem, smem, anywhere, vmem, vmem, vmem, vmem],
        out_specs=anywhere,
        scratch_shapes=[
            pltpu.VMEM((max(sizes) + 16, R), jnp.float32),
            pltpu.VMEM((FA, max(sizes), R), jnp.float32),
            pltpu.VMEM((rows, R), jnp.float32),
            pltpu.SemaphoreType.DMA((pieces,)),
            pltpu.SemaphoreType.DMA((pieces,)),
        ],
        compiler_params=pltpu.CompilerParams(vmem_limit_bytes=56 * MIB),
        cost_estimate=pl.CostEstimate(
            flops=2 * rows * R, bytes_accessed=8 * rows * R, transcendentals=0
        ),
        name="update",
    )(is_sea, column, part, rim, forcing, halo, mask)


def local(
    fields, atm_mixing, ocean_mixing, sea_mask, source_slot, target_tile, target_slot, remap_blocks
):
    n_comp = lax.axis_size("comp")
    n_tile = lax.axis_size("tile")
    is_sea = lax.axis_index("comp") == n_comp - 1
    sea_cols = sea_mask.shape[2]
    atm_cols = sea_cols * 5 // 6
    sizes = (atm_cols, sea_cols)
    sea_flag = is_sea.astype(jnp.int32).reshape(1)
    mask = sea_mask[0, 0].astype(jnp.float32)
    state = fields[0, 0]
    tiles = target_tile[0, 0, :, 0]
    weights = remap_blocks[0, 0]
    forward = [(i, (i + 1) % n_tile) for i in range(n_tile)]
    backward = [(b, a) for a, b in forward]

    def atm_edges(values):
        split = values.reshape(FA * LA, atm_cols // HALO, HALO, R)
        return split[:, 0], split[:, -1]

    def sea_edges(values):
        split = values.reshape(FO * LO, sea_cols // HALO, HALO, R)
        spare = FA * LA - FO * LO
        cut = mask.reshape(sea_cols // HALO, HALO, R)
        fill = lambda edge, own: jnp.concatenate(
            [edge, own[None], jnp.zeros((spare - 1, HALO, R), jnp.float32)], axis=0
        )
        return fill(split[:, 0], cut[0]), fill(split[:, -1], cut[-1])

    low_edge, high_edge = lax.cond(is_sea, sea_edges, atm_edges, state)
    low_edge, high_edge, tiles = lax.optimization_barrier((low_edge, high_edge, tiles))
    left = lax.ppermute(high_edge, "tile", forward)
    right = lax.ppermute(low_edge, "tile", backward)

    place = jnp.stack([is_sea.astype(jnp.int32), lax.axis_index("tile")])
    sent = remap(
        place,
        source_slot.reshape(1, -1),
        tiles.reshape(1, -1),
        target_slot.reshape(1, -1),
        state.reshape(-1, R),
        weights,
        n_tile,
        sizes,
    )
    received = lax.all_to_all(
        sent, "tile", split_axis=0, concat_axis=0, tiled=True
    )

    part = inner_dynamics(sea_flag, state.reshape(-1, R), atm_mixing, ocean_mixing, mask, sizes)
    mask_left, mask_right = left[FO * LO], right[FO * LO]
    work_mask = jnp.concatenate(
        [jnp.zeros((4, R), jnp.float32), mask_left, mask, mask_right, jnp.zeros((4, R), jnp.float32)], axis=0
    )
    rim = rim_dynamics(
        sea_flag,
        state.reshape(FA * LA, atm_cols, R),
        state.reshape(FO * LO, sea_cols, R),
        left.reshape(FA * LA * HALO, R),
        right.reshape(FA * LA * HALO, R),
        atm_mixing,
        ocean_mixing,
        work_mask[HALO:-HALO],
        sizes,
    )

    received, part = lax.optimization_barrier((received, part))
    shares = lax.all_to_all(combine(received, sea_cols), "comp", split_axis=0, concat_axis=0, tiled=True)
    pushed = COUPLE_RATE * jnp.sum(shares, axis=0) * mask
    low_part = pushed[:, :HALO]
    high_part = jnp.where(is_sea, pushed[:, sea_cols - HALO :], pushed[:, atm_cols - HALO : atm_cols])
    halo = jnp.stack(
        [lax.ppermute(high_part, "tile", forward), lax.ppermute(low_part, "tile", backward)]
    )
    atm_column = jnp.einsum(
        "flm,fm->fl", atm_mixing, atm_mixing[:, :, LA - 1], precision=lax.Precision.HIGHEST
    ).reshape(-1)
    ocean_column = jnp.einsum(
        "flm,fm->fl", ocean_mixing, ocean_mixing[:, :, 0], precision=lax.Precision.HIGHEST
    ).reshape(-1)
    ocean_column = jnp.pad(ocean_column, (0, FA * LA - FO * LO))
    column = jnp.where(is_sea, ocean_column, atm_column)
    done = update(sea_flag, column, part, rim, pushed, halo, work_mask, sizes)
    return done.reshape(1, 1, -1)


def solution(mesh):
    in_specs = (
        P("comp", "tile", None),
        P(),
        P(),
        P("comp", "tile", None, None),
        P("comp", "tile", None),
        P("comp", "tile", None, None),
        P("comp", "tile", None),
        P("comp", "tile", None, None, None),
    )
    out_specs = P("comp", "tile", None)
    return jax.shard_map(local, mesh=mesh, in_specs=in_specs, out_specs=out_specs, check_vma=False)
```

```python
import functools

import jax
import jax.numpy as jnp
import numpy as np
from jax import lax
from jax.experimental import pallas as pl
from jax.experimental.pallas import tpu as pltpu
from jax.sharding import PartitionSpec as P

FA = 3
FO = 4
LA = 128
LO = 80
R = 128
CAP = 16

COUPLE_RATE = 0.1
NU_ATMOS = 0.02
NU_OCEAN = 0.015

HALO = 4
EDGE_ROWS = 3 * 2 * HALO
FIELD_ROWS = CAP + EDGE_ROWS
CHUNK_ROWS = FA * FIELD_ROWS + 8
MIB = 1 << 20
SIDE = (4, 5)


def split_two(value):
    high = value.astype(jnp.bfloat16)
    return high, (value - high.astype(jnp.float32)).astype(jnp.bfloat16)


def row_operator():
    u = np.eye(R, k=1) + np.eye(R, k=-1) - 4.0 * np.eye(R)
    both = np.concatenate([2.0 * u, u @ u + 2.0 * np.eye(R)], axis=1)
    return jnp.asarray(np.concatenate([both, both], axis=0), jnp.bfloat16)


def apply_filter(value, column_sums, row_parts, nu):
    return value - nu * (column_sums + row_parts)


def filter_planes(column, first, last, nu, mask, operator, lhs_ref, emit):
    rows = 16
    for k in range(first - 1, last + 1):
        spot = (k - first + 1) * rows
        high, low = split_two(column(k))
        lhs_ref[spot : spot + rows, :R] = high
        lhs_ref[spot : spot + rows, R:] = low
    both = jnp.dot(
        lhs_ref[: (last - first + 2) * rows], operator, preferred_element_type=jnp.float32
    )

    def part(k, half):
        spot = (k - first + 1) * rows
        return both[spot : spot + rows, half * R : (half + 1) * R]

    for k in range(first, last):
        column_sums = column(k - 2) + column(k + 2)
        row_parts = (part(k - 1, 0) + part(k + 1, 0)) + part(k, 1)
        plane = apply_filter(column(k), column_sums, row_parts, nu)
        if mask is not None:
            plane = plane * mask(k)
        emit(k, plane)


def surface_copies(sizes, sea, x_ref, surf_ref, sems):
    atm_cols, sea_cols = sizes
    if sea:
        cols, starts = sea_cols, [f * LO * sea_cols for f in range(FA)]
    else:
        cols, starts = atm_cols, [(f * LA + LA - 1) * atm_cols for f in range(FA)]
    return [
        pltpu.make_async_copy(
            x_ref.at[pl.ds(start, cols)], surf_ref.at[pl.ds(f * sea_cols, cols)], sems.at[f]
        )
        for f, start in enumerate(starts)
    ]


def small_mod(value, modulus, limit):
    for step in range(modulus, limit, modulus):
        value = jnp.where(value >= modulus, value - modulus, value)
    return value


def as_column(row):
    n = row.shape[1]
    diagonal = lax.broadcasted_iota(jnp.int32, (n, n), 0) == lax.broadcasted_iota(jnp.int32, (n, n), 1)
    return jnp.sum(jnp.where(diagonal, row, 0.0), axis=1, keepdims=True)


def ones_where(condition):
    return jnp.where(condition, 1.0, 0.0).astype(jnp.bfloat16)


def remap_kernel(
    sizes, n_tile, chunks, sea_ref, place_ref, source_ref, tile_ref, slot_ref, x_ref, w_ref, out_ref, w_vmem, surf_ref, pick_ref, part_ref, w_sems, x_sems
):
    atm_cols, sea_cols = sizes
    entries = source_ref.shape[1]
    quarter = entries // 4
    per_chunk = quarter // chunks
    code_limit = 5 * sea_cols
    copies = [
        pltpu.make_async_copy(
            w_ref.at[:, pl.ds(n * per_chunk, per_chunk)], w_vmem.at[:, pl.ds(n * per_chunk, per_chunk)], w_sems.at[n]
        )
        for n in range(chunks)
    ]
    is_sea = sea_ref[0] != 0
    for sea in (False, True):

        @pl.when(is_sea == sea)
        def _(sea=sea):
            for copy in surface_copies(sizes, sea, x_ref, surf_ref, x_sems):
                copy.start()

    for copy in copies:
        copy.start()

    tile = tile_ref[...].astype(jnp.float32)
    tile_column = as_column(tile)
    earlier = lax.broadcasted_iota(jnp.int32, (entries, entries), 0) < lax.broadcasted_iota(
        jnp.int32, (entries, entries), 1
    )
    rank = jnp.sum(jnp.where((tile_column == tile) & earlier, 1.0, 0.0), axis=0, keepdims=True)
    code = slot_ref[...]
    for_atm = small_mod(code, 3 * atm_cols, code_limit)
    for_atm_block = small_mod(for_atm, atm_cols, 3 * atm_cols)
    for_atm_group = jnp.where(for_atm >= atm_cols, 1, 0) + jnp.where(for_atm >= 2 * atm_cols, 1, 0)
    for_sea_block = small_mod(code, sea_cols, code_limit)
    window = sea_cols + 2 * HALO
    group = jnp.where(is_sea, for_atm_group, 3)
    block = jnp.where(is_sea, for_atm_block, for_sea_block)
    dest = (group * window + block + HALO + 1).astype(jnp.float32)
    lane = rank + (CAP * lax.rem(place_ref[0], R // CAP)).astype(jnp.float32)
    spots = lax.broadcasted_iota(jnp.int32, (R, entries), 0).astype(jnp.float32)
    marks = jnp.where(spots == lane, dest, 0.0).astype(jnp.bfloat16)
    tiles = lax.broadcasted_iota(jnp.int32, (n_tile, entries), 0).astype(jnp.float32)
    codes = lax.dot_general(
        ones_where(tiles == tile), marks, (((1,), (1,)), ((), ())), preferred_element_type=jnp.float32
    )
    tile_number = tile_ref[...]
    high_start = jnp.where(is_sea, atm_cols, sea_cols) - HALO
    edge_tile = jnp.where(block < HALO, tile_number + n_tile - 1, tile_number + 1)
    edge_tile = jnp.where(edge_tile >= n_tile, edge_tile - n_tile, edge_tile)
    edge_row = jnp.where(block < HALO, block + HALO, block - high_start)
    edge_row = edge_tile * EDGE_ROWS + jnp.where(is_sea, group, 0) * (2 * HALO) + edge_row
    on_edge = (block < HALO) | (block >= high_start)
    edge_slot = jnp.where(on_edge, edge_row, -1).astype(jnp.float32)
    tail = CHUNK_ROWS - FA * FIELD_ROWS
    for t in range(n_tile):
        out_ref[t, FA * FIELD_ROWS :, :] = jnp.concatenate(
            [codes[t : t + 1], jnp.zeros((tail - 1, R), jnp.float32)], axis=0
        )

    source = source_ref[...]
    source = jnp.where(
        is_sea, small_mod(source, sea_cols, code_limit), small_mod(source, atm_cols, code_limit)
    )
    source_column = as_column(source.astype(jnp.float32))
    columns = lax.broadcasted_iota(jnp.int32, (entries, sea_cols), 1).astype(jnp.float32)
    chooser = ones_where(columns == source_column)
    for sea in (False, True):

        @pl.when(is_sea == sea)
        def _(sea=sea):
            for copy in surface_copies(sizes, sea, x_ref, surf_ref, x_sems):
                copy.wait()
            if not sea:
                for f in range(FA):
                    surf_ref[f * sea_cols + atm_cols : (f + 1) * sea_cols, :] = jnp.zeros(
                        (sea_cols - atm_cols, R), jnp.float32
                    )

    for f in range(FA):
        surface = surf_ref[f * sea_cols : (f + 1) * sea_cols, :].astype(jnp.bfloat16)
        pick_ref[f * entries : (f + 1) * entries, :] = jnp.dot(
            chooser, surface, preferred_element_type=jnp.float32
        )
    pick_ref[FA * entries :, :] = jnp.zeros((entries, R), jnp.float32)

    member = lax.rem(lax.broadcasted_iota(jnp.int32, (16, R), 0), 4)
    def chunk(n, carry):
        span = pl.ds(n * per_chunk, per_chunk)
        pltpu.make_async_copy(w_ref.at[:, span], w_vmem.at[:, span], w_sems.at[n]).wait()
        for step in range(per_chunk):
            g = n * per_chunk + step
            picked = pick_ref[pl.ds(g, 16, stride=quarter), :]
            rows = jnp.concatenate(
                [jnp.where(member < 2, picked, 0.0), jnp.where(member >= 2, picked, 0.0)], axis=1
            ).astype(jnp.bfloat16)
            block = jnp.concatenate(
                [
                    jnp.concatenate([w_vmem[0, g], w_vmem[2, g]], axis=1),
                    jnp.concatenate([w_vmem[1, g], w_vmem[3, g]], axis=1),
                ],
                axis=0,
            )
            res = lax.dot_general(
                rows, block, (((1,), (1,)), ((), ())), preferred_element_type=jnp.float32
            )
            part_ref[pl.ds(g, 16, stride=quarter), :] = jnp.where(member % 2 == 0, res[:, :R], res[:, R:])
        return carry

    lax.fori_loop(0, chunks, chunk, 0)

    slot = tile * CAP + rank
    slots = lax.broadcasted_iota(jnp.int32, (n_tile * CAP, entries), 0).astype(jnp.float32)
    placer = ones_where(slots == slot)
    edge_slots = lax.broadcasted_iota(jnp.int32, (n_tile * EDGE_ROWS, entries), 0).astype(jnp.float32)
    edge_placer = ones_where(edge_slots == edge_slot)
    for f in range(FA):
        high, low = split_two(part_ref[f * entries : (f + 1) * entries, :])
        values = jnp.concatenate([high, low], axis=1)
        start = f * FIELD_ROWS
        for place_matrix, size in ((placer, CAP), (edge_placer, EDGE_ROWS)):
            both = jnp.dot(place_matrix, values, preferred_element_type=jnp.float32)
            placed = both[:, :R] + both[:, R:]
            for t in range(n_tile):
                out_ref[t, start : start + size, :] = placed[t * size : (t + 1) * size]
            start += size


def remap(is_sea, place, source, tile, slot, x, weights, n_tile, sizes):
    entries = weights.shape[0]
    chunks = 8
    vmem = pl.BlockSpec(memory_space=pltpu.VMEM)
    anywhere = pl.BlockSpec(memory_space=pl.ANY)
    return pl.pallas_call(
        functools.partial(remap_kernel, sizes, n_tile, chunks),
        out_shape=jax.ShapeDtypeStruct((n_tile, CHUNK_ROWS, R), jnp.float32),
        in_specs=[pl.BlockSpec(memory_space=pltpu.SMEM)] * 2 + [vmem, vmem, vmem, anywhere, anywhere],
        out_specs=vmem,
        scratch_shapes=[
            pltpu.VMEM((4, entries // 4, R, R), jnp.bfloat16),
            pltpu.VMEM((FA * sizes[1], R), jnp.float32),
            pltpu.VMEM((4 * entries, R), jnp.float32),
            pltpu.VMEM((4 * entries, R), jnp.float32),
            pltpu.SemaphoreType.DMA((chunks,)),
            pltpu.SemaphoreType.DMA((FA,)),
        ],
        compiler_params=pltpu.CompilerParams(vmem_limit_bytes=56 * MIB),
        cost_estimate=pl.CostEstimate(
            flops=2000 * entries * R * R, bytes_accessed=weights.size * 2, transcendentals=0
        ),
        name="remap",
    )(is_sea, place, source, tile, slot, x, weights.reshape(4, entries // 4, R, R))


def combine_kernel(sizes, sea_ref, recv_ref, out_ref):
    atm_cols, sea_cols = sizes
    n_tile, per_group = recv_ref.shape[0], out_ref.shape[2]
    rows = 4 * per_group
    spots = lax.broadcasted_iota(jnp.int32, (rows, R), 0).astype(jnp.float32) + 1.0
    total = [jnp.zeros((rows, R), jnp.float32) for _ in range(FA)]
    for g in range(n_tile // 8):
        some = slice(g * 8, (g + 1) * 8)
        code = jnp.sum(recv_ref[some, FA * FIELD_ROWS, :], axis=0, keepdims=True)
        pick = ones_where(spots == code)
        for f in range(FA):
            start = f * FIELD_ROWS
            high, low = split_two(recv_ref[some, start : start + CAP, :].reshape(8 * CAP, R))
            both = jnp.dot(
                pick, jnp.concatenate([high, low], axis=1), preferred_element_type=jnp.float32
            )
            total[f] = total[f] + (both[:, :R] + both[:, R:])
    for f in range(FA):
        for c in range(4):
            out_ref[c, f] = total[f][c * per_group : (c + 1) * per_group]
    for f in range(FA):
        start = f * FIELD_ROWS + CAP
        edge = jnp.sum(recv_ref[:, start : start + EDGE_ROWS, :], axis=0)

        @pl.when(sea_ref[0] == 0)
        def _(f=f, edge=edge):
            out_ref[3, f, 0:HALO, :] = edge[0:HALO]
            out_ref[3, f, HALO + sea_cols : 2 * HALO + sea_cols, :] = edge[HALO : 2 * HALO]

        @pl.when(sea_ref[0] != 0)
        def _(f=f, edge=edge):
            for c in range(3):
                first = c * 2 * HALO
                out_ref[c, f, 0:HALO, :] = edge[first : first + HALO]
                out_ref[c, f, HALO + atm_cols : 2 * HALO + atm_cols, :] = edge[first + HALO : first + 2 * HALO]


def combine(is_sea, recv, sizes):
    vmem = pl.BlockSpec(memory_space=pltpu.VMEM)
    return pl.pallas_call(
        functools.partial(combine_kernel, sizes),
        out_shape=jax.ShapeDtypeStruct((4, FA, sizes[1] + 2 * HALO, R), jnp.float32),
        in_specs=[pl.BlockSpec(memory_space=pltpu.SMEM), vmem],
        out_specs=vmem,
        compiler_params=pltpu.CompilerParams(vmem_limit_bytes=16 * MIB),
        name="combine",
    )(is_sea, recv)


def edges_kernel(sea_ref, x_atm_ref, x_sea_ref, mask_ref, low_ref, high_ref, sems):
    for sea, x_ref in ((False, x_atm_ref), (True, x_sea_ref)):
        count, blocks = x_ref.shape[0], x_ref.shape[1]

        @pl.when((sea_ref[0] != 0) == sea)
        def _(sea=sea, x_ref=x_ref, count=count, blocks=blocks):
            copies = [
                pltpu.make_async_copy(x_ref.at[:, 0], low_ref.at[pl.ds(0, count)], sems.at[0]),
                pltpu.make_async_copy(x_ref.at[:, blocks - 1], high_ref.at[pl.ds(0, count)], sems.at[1]),
            ]
            for copy in copies:
                copy.start()
            for ref, block in ((low_ref, 0), (high_ref, blocks - 1)):
                if count < FA * LA:
                    ref[count : FA * LA] = jnp.zeros((FA * LA - count, HALO, R), jnp.float32)
                ref[FA * LA : FA * LA + 1] = mask_ref[block : block + 1].astype(jnp.float32)
                ref[FA * LA + 1 :] = jnp.zeros((ref.shape[0] - FA * LA - 1, HALO, R), jnp.float32)
            for copy in copies:
                copy.wait()


def edge_columns(is_sea, state, mask, sizes):
    atm_cols, sea_cols = sizes
    anywhere = pl.BlockSpec(memory_space=pl.ANY)
    vmem = pl.BlockSpec(memory_space=pltpu.VMEM)
    shape = jax.ShapeDtypeStruct((FA * LA + 2, HALO, R), jnp.float32)
    return pl.pallas_call(
        edges_kernel,
        out_shape=[shape, shape],
        in_specs=[pl.BlockSpec(memory_space=pltpu.SMEM), anywhere, anywhere, vmem],
        out_specs=[vmem, vmem],
        scratch_shapes=[pltpu.SemaphoreType.DMA((2,))],
        compiler_params=pltpu.CompilerParams(vmem_limit_bytes=56 * MIB),
        name="edges",
    )(
        is_sea,
        state.reshape(FA * LA, atm_cols // HALO, HALO, R),
        state.reshape(FO * LO, sea_cols // HALO, HALO, R),
        mask.reshape(sea_cols // HALO, HALO, R),
    )


def filtered_twice(cols, nu, column, mask, operator, lhs_ref, mid_ref, store):
    def middle(k):
        return mid_ref[(k + 2) * 16 : (k + 3) * 16, :]

    def keep(k, plane):
        mid_ref[(k + 2) * 16 : (k + 3) * 16, :] = plane

    filter_planes(column, -2, cols + 2, nu, mask, operator, lhs_ref.at[0], keep)
    filter_planes(middle, 0, cols, nu, mask, operator, lhs_ref.at[1], store)


def dynamics_part(
    fields, levels, cols, surface, side, nu, x_ref, left_ref, right_ref, matrix_ref, mask_ref, op_ref, out_ref, column_ref,
    x_vmem, out_vmem, y_vmem, lhs_ref, mid_ref, mask_vmem, in_sems, out_sems
):
    rows = levels * cols

    def read(f):
        span = pl.ds(pl.multiple_of(f * rows, 8), rows)
        return pltpu.make_async_copy(x_ref.at[span], x_vmem.at[span], in_sems.at[f])

    def write(f):
        span = pl.ds(pl.multiple_of(f * rows, 8), rows)
        return pltpu.make_async_copy(out_vmem.at[span], out_ref.at[span], out_sems.at[f])

    read(0).start()
    mask = None
    if mask_ref is not None:
        spare = FA * LA * HALO
        mask_vmem[0:HALO, :] = left_ref[spare : spare + HALO, :]
        mask_vmem[HALO : HALO + cols, :] = mask_ref[...].astype(jnp.float32)
        mask_vmem[HALO + cols : 2 * HALO + cols, :] = right_ref[spare : spare + HALO, :]
        mask = lambda k: jnp.broadcast_to(mask_vmem[k + HALO : k + HALO + 1, :], (16, R))

    def field(f, carry):
        squared = jnp.dot(
            matrix_ref[f], matrix_ref[f], precision=lax.Precision.HIGHEST, preferred_element_type=jnp.float32
        )
        column_ref[pl.ds(pl.multiple_of(f * levels, 8), levels), :] = jnp.broadcast_to(
            squared[:, surface : surface + 1], (levels, R)
        )
        high, low = split_two(squared)
        stacked = jnp.concatenate(
            [jnp.concatenate([high, high], axis=1), jnp.concatenate([low, jnp.zeros_like(low)], axis=1)], axis=0
        )
        read(f).wait()

        @pl.when(f + 1 < fields)
        def _():
            read(f + 1).start()

        def filter_rows(i, slot):
            first = f * levels + i * 16
            spot = pl.multiple_of(i * 16, 16)

            def column(k):
                if k < 0:
                    return left_ref[pl.ds(first * HALO + k + HALO, 16, stride=HALO), :]
                if k >= cols:
                    return right_ref[pl.ds(first * HALO + k - cols, 16, stride=HALO), :]
                return x_vmem[pl.ds(first * cols + k, 16, stride=cols), :]

            def store(k, plane):
                high, low = split_two(plane)
                y_vmem[pl.ds(spot, 16), k * R : (k + 1) * R] = high
                y_vmem[pl.ds(levels + spot, 16), k * R : (k + 1) * R] = low

            filtered_twice(cols, nu, column, mask, op_ref[...], lhs_ref.at[slot], mid_ref.at[slot], store)

        def filter_some(n, carry):
            for slot in range(side):
                filter_rows(n * side + slot, slot)
            return carry

        lax.fori_loop(0, levels // 16 // side, filter_some, 0)

        for pair in range(cols // 2):
            both = jnp.dot(
                stacked,
                y_vmem[: 2 * levels, 2 * pair * R : 2 * (pair + 1) * R],
                preferred_element_type=jnp.float32,
            )
            mixed = both[:levels] + both[levels:]
            for h in range(2):
                out_vmem[pl.ds(f * rows + 2 * pair + h, levels, stride=cols), :] = mixed[:, h * R : (h + 1) * R]
        write(f).start()
        return carry

    lax.fori_loop(0, fields, field, 0)
    for f in range(fields):
        write(f).wait()


def dynamics_kernel(
    sizes, sea_ref, x_ref, left_ref, right_ref, atm_ref, ocean_ref, mask_ref, op_ref, *rest
):
    atm_cols, sea_cols = sizes

    @pl.when(sea_ref[0] == 0)
    def _():
        dynamics_part(
            FA, LA, atm_cols, LA - 1, SIDE[0], NU_ATMOS, x_ref, left_ref, right_ref, atm_ref, None, op_ref, *rest
        )

    @pl.when(sea_ref[0] != 0)
    def _():
        dynamics_part(
            FO, LO, sea_cols, 0, SIDE[1], NU_OCEAN, x_ref, left_ref, right_ref, ocean_ref, mask_ref, op_ref, *rest
        )


def dynamics(is_sea, x, left, right, atm_mixing, ocean_mixing, mask, sizes):
    vmem = pl.BlockSpec(memory_space=pltpu.VMEM)
    anywhere = pl.BlockSpec(memory_space=pl.ANY)
    rows = x.shape[0]
    widest = max(sizes)
    return pl.pallas_call(
        functools.partial(dynamics_kernel, sizes),
        out_shape=[
            jax.ShapeDtypeStruct((rows, R), jnp.float32),
            jax.ShapeDtypeStruct((FA * LA, R), jnp.float32),
        ],
        in_specs=[pl.BlockSpec(memory_space=pltpu.SMEM), anywhere] + [vmem] * 6,
        out_specs=[anywhere, vmem],
        scratch_shapes=[
            pltpu.VMEM((rows, R), jnp.float32),
            pltpu.VMEM((rows, R), jnp.float32),
            pltpu.VMEM((2 * LA, widest * R), jnp.bfloat16),
            pltpu.VMEM((max(SIDE), 2, (widest + 6) * 16, 2 * R), jnp.bfloat16),
            pltpu.VMEM((max(SIDE), (widest + 4) * 16, R), jnp.float32),
            pltpu.VMEM((widest + 2 * HALO, R), jnp.float32),
            pltpu.SemaphoreType.DMA((FO,)),
            pltpu.SemaphoreType.DMA((FO,)),
        ],
        compiler_params=pltpu.CompilerParams(vmem_limit_bytes=56 * MIB),
        cost_estimate=pl.CostEstimate(
            flops=100 * rows * R * R, bytes_accessed=16 * rows * R, transcendentals=0
        ),
        name="dynamics",
    )(is_sea, x, left, right, atm_mixing, ocean_mixing, mask, row_operator())


def lane_edges(rows):
    lane = lax.broadcasted_iota(jnp.int32, (rows, R), 1)
    return lane == 0, lane == R - 1


def lap(before, middle, after, edges):
    first, last = edges
    down = jnp.where(first, 0.0, pltpu.roll(middle, 1, 1))
    up = jnp.where(last, 0.0, pltpu.roll(middle, R - 1, 1))
    return (before + after) + (down + up) - 4.0 * middle


def filter_forcing(cols, nu, shares_ref, masked, mask_ref, work_ref, g_ref):
    lo, hi, rows = 8, 8 + cols, cols + 16
    edges = lane_edges(rows)
    mask = mask_ref[0:rows, :]

    def along(v):
        return lap(pltpu.roll(v, 1, 0), v, pltpu.roll(v, rows - 1, 0), edges)

    for f in range(FA):
        forcing = (shares_ref[0, f] + shares_ref[1, f]) + (shares_ref[2, f] + shares_ref[3, f])
        work_ref[0:rows, :] = jnp.zeros((rows, R), jnp.float32)
        work_ref[lo - HALO : hi + HALO, :] = COUPLE_RATE * forcing[: cols + 2 * HALO]
        value = work_ref[0:rows, :] * mask
        for _ in range(2):
            value = value - nu * along(along(value))
            if masked:
                value = value * mask
        g_ref[f, :cols] = value[lo:hi]


def update_part(
    cols, levels, fields, pieces, masked, nu, column_ref, part_ref, shares_ref, mask_ref, left_ref, right_ref, out_ref,
    work_ref, g_ref, mask_vmem, stage_ref, in_sems, out_sems, mask_sems
):
    per_piece = fields * levels // pieces
    rows = per_piece * cols

    def read(p):
        span = pl.ds(pl.multiple_of(p * rows, 8), rows)
        return pltpu.make_async_copy(part_ref.at[span], stage_ref.at[span], in_sems.at[p])

    def write(p):
        span = pl.ds(pl.multiple_of(p * rows, 8), rows)
        return pltpu.make_async_copy(stage_ref.at[span], out_ref.at[span], out_sems.at[p])

    span = pl.ds(FA * LA * HALO, 8)
    ends = [
        pltpu.make_async_copy(left_ref.at[span], mask_vmem.at[pl.ds(64, 8)], mask_sems.at[0]),
        pltpu.make_async_copy(right_ref.at[span], mask_vmem.at[pl.ds(72, 8)], mask_sems.at[1]),
    ]
    for copy in ends:
        copy.start()
    for p in range(pieces):
        read(p).start()
    mask_vmem[0:8, :] = jnp.zeros((8, R), jnp.float32)
    mask_vmem[8 : 8 + cols, :] = mask_ref[:cols].astype(jnp.float32)
    mask_vmem[8 + cols : 16 + cols, :] = jnp.zeros((8, R), jnp.float32)
    for copy in ends:
        copy.wait()
    mask_vmem[8 - HALO : 8, :] = mask_vmem[64 : 64 + HALO, :]
    mask_vmem[8 + cols : 8 + HALO + cols, :] = mask_vmem[72 : 72 + HALO, :]
    filter_forcing(cols, nu, shares_ref, masked, mask_vmem, work_ref, g_ref)

    def piece(p, carry):
        read(p).wait()
        field = p * per_piece // levels

        @pl.when(field < FA)
        def _():
            pushed = [g_ref[field, v * 8 : v * 8 + 8, :] for v in range(cols // 8)]

            def group(q, carry):
                number = p * per_piece + q
                factor = jnp.broadcast_to(column_ref[pl.ds(number, 1), :], (8, R))
                for v in range(cols // 8):
                    span = pl.ds(pl.multiple_of(number * cols + v * 8, 8), 8)
                    stage_ref[span, :] = stage_ref[span, :] + factor * pushed[v]
                return carry

            lax.fori_loop(0, per_piece, group, 0, unroll=8)

        write(p).start()
        return carry

    lax.fori_loop(0, pieces, piece, 0)
    for p in range(pieces):
        write(p).wait()


def update_kernel(sizes, sea_ref, *rest):
    atm_cols, sea_cols = sizes

    @pl.when(sea_ref[0] == 0)
    def _():
        update_part(atm_cols, LA, FA, 4 * FA, False, NU_ATMOS, *rest)

    @pl.when(sea_ref[0] != 0)
    def _():
        update_part(sea_cols, LO, FO, 2 * FO, True, NU_OCEAN, *rest)


def update(is_sea, column, part, shares, mask, left, right, sizes):
    vmem = pl.BlockSpec(memory_space=pltpu.VMEM)
    smem = pl.BlockSpec(memory_space=pltpu.SMEM)
    anywhere = pl.BlockSpec(memory_space=pl.ANY)
    rows = part.shape[0]
    return pl.pallas_call(
        functools.partial(update_kernel, sizes),
        out_shape=jax.ShapeDtypeStruct((rows, R), jnp.float32),
        in_specs=[smem, vmem, anywhere, vmem, vmem, anywhere, anywhere],
        out_specs=anywhere,
        scratch_shapes=[
            pltpu.VMEM((max(sizes) + 16, R), jnp.float32),
            pltpu.VMEM((FA, max(sizes), R), jnp.float32),
            pltpu.VMEM((80, R), jnp.float32),
            pltpu.VMEM((rows, R), jnp.float32),
            pltpu.SemaphoreType.DMA((4 * FA,)),
            pltpu.SemaphoreType.DMA((4 * FA,)),
            pltpu.SemaphoreType.DMA((2,)),
        ],
        compiler_params=pltpu.CompilerParams(vmem_limit_bytes=56 * MIB),
        cost_estimate=pl.CostEstimate(
            flops=2 * rows * R, bytes_accessed=8 * rows * R, transcendentals=0
        ),
        name="update",
    )(is_sea, column, part, shares, mask, left, right)


def local(
    fields, atm_mixing, ocean_mixing, sea_mask, source_slot, target_tile, target_slot, remap_blocks
):
    n_comp = lax.axis_size("comp")
    n_tile = lax.axis_size("tile")
    is_sea = lax.axis_index("comp") == n_comp - 1
    sea_cols = sea_mask.shape[2]
    atm_cols = sea_cols * 5 // 6
    sizes = (atm_cols, sea_cols)
    sea_flag = is_sea.astype(jnp.int32).reshape(1)
    mask = sea_mask[0, 0]
    state = fields[0, 0]
    tiles = target_tile[0, 0, :, 0]
    weights = remap_blocks[0, 0]
    forward = [(i, (i + 1) % n_tile) for i in range(n_tile)]
    backward = [(b, a) for a, b in forward]

    low_edge, high_edge = edge_columns(sea_flag, state, mask, sizes)
    low_edge, high_edge, tiles = lax.optimization_barrier((low_edge, high_edge, tiles))
    left = lax.ppermute(high_edge, "tile", forward)
    right = lax.ppermute(low_edge, "tile", backward)

    sent = remap(
        sea_flag,
        lax.axis_index("tile").reshape(1),
        source_slot.reshape(1, -1),
        tiles.reshape(1, -1),
        target_slot.reshape(1, -1),
        state.reshape(-1, R),
        weights,
        n_tile,
        sizes,
    )
    received = lax.all_to_all(
        sent, "tile", split_axis=0, concat_axis=0, tiled=True
    )

    x = state.reshape(-1, R)
    flat_left = left.reshape(-1, R)
    flat_right = right.reshape(-1, R)
    part, column = dynamics(sea_flag, x, flat_left, flat_right, atm_mixing, ocean_mixing, mask, sizes)

    received, part = lax.optimization_barrier((received, part))
    shares = lax.all_to_all(combine(sea_flag, received, sizes), "comp", split_axis=0, concat_axis=0, tiled=True)
    done = update(sea_flag, column, part, shares, mask, flat_left, flat_right, sizes)
    return done.reshape(1, 1, -1)


def solution(mesh):
    in_specs = (
        P("comp", "tile", None),
        P(),
        P(),
        P("comp", "tile", None, None),
        P("comp", "tile", None),
        P("comp", "tile", None, None),
        P("comp", "tile", None),
        P("comp", "tile", None, None, None),
    )
    out_specs = P("comp", "tile", None)
    return jax.shard_map(local, mesh=mesh, in_specs=in_specs, out_specs=out_specs, check_vma=False)
```

```python
import functools

import jax
import jax.numpy as jnp
from jax import lax
from jax.experimental import pallas as pl
from jax.experimental.pallas import tpu as pltpu
from jax.sharding import PartitionSpec as P

FA = 3
FO = 4
LA = 128
LO = 80
R = 128
CAP = 16

COUPLE_RATE = 0.1
NU_ATMOS = 0.02
NU_OCEAN = 0.015

HALO = 4
EDGE_ROWS = 2 * HALO
FIELD_ROWS = CAP + EDGE_ROWS
MAIN_ROWS = FA * FIELD_ROWS + 8
CHUNK_ROWS = MAIN_ROWS + FA * EDGE_ROWS
MIB = 1 << 20
LIMIT = 52
SIDE = (8, 5)


def split_two(value):
    high = value.astype(jnp.bfloat16)
    return high, (value - high.astype(jnp.float32)).astype(jnp.bfloat16)


def row_operator():
    row = lax.broadcasted_iota(jnp.int32, (R, R), 0)
    lane = lax.broadcasted_iota(jnp.int32, (R, R), 1)
    apart = jnp.abs(row - lane)
    u = jnp.where(apart == 0, -4.0, jnp.where(apart == 1, 1.0, 0.0))
    ends = jnp.where((row == 0) | (row == R - 1), 1.0, 0.0)
    squared = jnp.where(apart == 1, -8.0, jnp.where(apart == 2, 1.0, 0.0))
    squared = jnp.where(apart == 0, 20.0 - ends, squared)
    both = jnp.concatenate([2.0 * u, squared], axis=1).astype(jnp.bfloat16)
    return jnp.concatenate([both, both], axis=0)


def apply_filter(value, column_sums, row_parts, nu):
    return value - nu * (column_sums + row_parts)


def filter_planes(column, first, last, nu, mask, operator, lhs_ref, emit):
    rows = 16
    for k in range(first - 1, last + 1):
        spot = (k - first + 1) * rows
        high, low = split_two(column(k))
        lhs_ref[spot : spot + rows, :R] = high
        lhs_ref[spot : spot + rows, R:] = low
    both = jnp.dot(
        lhs_ref[: (last - first + 2) * rows], operator, preferred_element_type=jnp.float32
    )

    def part(k, half):
        spot = (k - first + 1) * rows
        return both[spot : spot + rows, half * R : (half + 1) * R]

    for k in range(first, last):
        column_sums = column(k - 2) + column(k + 2)
        row_parts = (part(k - 1, 0) + part(k + 1, 0)) + part(k, 1)
        plane = apply_filter(column(k), column_sums, row_parts, nu)
        if mask is not None:
            plane = plane * mask(k)
        emit(k, plane)


def surface_copies(sizes, sea, x_ref, surf_ref, sems):
    atm_cols, sea_cols = sizes
    if sea:
        cols, starts = sea_cols, [f * LO * sea_cols for f in range(FA)]
    else:
        cols, starts = atm_cols, [(f * LA + LA - 1) * atm_cols for f in range(FA)]
    return [
        pltpu.make_async_copy(
            x_ref.at[pl.ds(start, cols)], surf_ref.at[pl.ds(f * sea_cols, cols)], sems.at[f]
        )
        for f, start in enumerate(starts)
    ]


def small_mod(value, modulus, limit):
    for step in range(modulus, limit, modulus):
        value = jnp.where(value >= modulus, value - modulus, value)
    return value


def as_column(row):
    n = row.shape[1]
    diagonal = lax.broadcasted_iota(jnp.int32, (n, n), 0) == lax.broadcasted_iota(jnp.int32, (n, n), 1)
    return jnp.sum(jnp.where(diagonal, row, 0.0), axis=1, keepdims=True)


def ones_where(condition):
    return jnp.where(condition, 1.0, 0.0).astype(jnp.bfloat16)


def remap_kernel(
    sizes, n_tile, chunks, sea_ref, place_ref, source_ref, tile_ref, slot_ref, x_ref, w_ref, out_ref, third_ref, w_vmem, surf_ref, pick_ref, part_ref, w_sems, x_sems
):
    atm_cols, sea_cols = sizes
    entries = source_ref.shape[1]
    quarter = entries // 4
    per_chunk = quarter // chunks
    code_limit = 5 * sea_cols
    copies = [
        pltpu.make_async_copy(
            w_ref.at[:, pl.ds(n * per_chunk, per_chunk)], w_vmem.at[:, pl.ds(n * per_chunk, per_chunk)], w_sems.at[n]
        )
        for n in range(chunks)
    ]
    is_sea = sea_ref[0] != 0
    for sea in (False, True):

        @pl.when(is_sea == sea)
        def _(sea=sea):
            for copy in surface_copies(sizes, sea, x_ref, surf_ref, x_sems):
                copy.start()

    for copy in copies:
        copy.start()

    tile = tile_ref[...].astype(jnp.float32)
    tile_column = as_column(tile)
    earlier = lax.broadcasted_iota(jnp.int32, (entries, entries), 0) < lax.broadcasted_iota(
        jnp.int32, (entries, entries), 1
    )
    rank = jnp.sum(jnp.where((tile_column == tile) & earlier, 1.0, 0.0), axis=0, keepdims=True)
    code = slot_ref[...]
    for_atm = small_mod(code, 3 * atm_cols, code_limit)
    for_atm_block = small_mod(for_atm, atm_cols, 3 * atm_cols)
    for_atm_group = jnp.where(for_atm >= atm_cols, 1, 0) + jnp.where(for_atm >= 2 * atm_cols, 1, 0)
    for_sea_block = small_mod(code, sea_cols, code_limit)
    window = sea_cols + 2 * HALO
    group = jnp.where(is_sea, for_atm_group, 3)
    block = jnp.where(is_sea, for_atm_block, for_sea_block)
    dest = (group * window + block + HALO + 1).astype(jnp.float32)
    lane = rank + (CAP * lax.rem(place_ref[0], R // CAP)).astype(jnp.float32)
    spots = lax.broadcasted_iota(jnp.int32, (R, entries), 0).astype(jnp.float32)
    marks = jnp.where(spots == lane, dest, 0.0).astype(jnp.bfloat16)
    tiles = lax.broadcasted_iota(jnp.int32, (n_tile, entries), 0).astype(jnp.float32)
    codes = lax.dot_general(
        ones_where(tiles == tile), marks, (((1,), (1,)), ((), ())), preferred_element_type=jnp.float32
    )
    tile_number = tile_ref[...]
    high_start = jnp.where(is_sea, atm_cols, sea_cols) - HALO
    edge_tile = jnp.where(block < HALO, tile_number + n_tile - 1, tile_number + 1)
    edge_tile = jnp.where(edge_tile >= n_tile, edge_tile - n_tile, edge_tile)
    edge_row = jnp.where(block < HALO, block + HALO, block - high_start)
    edge_row = (jnp.where(is_sea, group, 0) * n_tile + edge_tile) * EDGE_ROWS + edge_row
    on_edge = (block < HALO) | (block >= high_start)
    edge_slot = jnp.where(on_edge, edge_row, -1).astype(jnp.float32)
    tail = MAIN_ROWS - FA * FIELD_ROWS
    for t in range(n_tile):
        out_ref[t, FA * FIELD_ROWS : MAIN_ROWS, :] = jnp.concatenate(
            [codes[t : t + 1], jnp.zeros((tail - 1, R), jnp.float32)], axis=0
        )

    source = source_ref[...]
    source = jnp.where(
        is_sea, small_mod(source, sea_cols, code_limit), small_mod(source, atm_cols, code_limit)
    )
    source_column = as_column(source.astype(jnp.float32))
    columns = lax.broadcasted_iota(jnp.int32, (entries, sea_cols), 1).astype(jnp.float32)
    chooser = ones_where(columns == source_column)
    for sea in (False, True):

        @pl.when(is_sea == sea)
        def _(sea=sea):
            for copy in surface_copies(sizes, sea, x_ref, surf_ref, x_sems):
                copy.wait()
            if not sea:
                for f in range(FA):
                    surf_ref[f * sea_cols + atm_cols : (f + 1) * sea_cols, :] = jnp.zeros(
                        (sea_cols - atm_cols, R), jnp.float32
                    )

    for f in range(FA):
        surface = surf_ref[f * sea_cols : (f + 1) * sea_cols, :].astype(jnp.bfloat16)
        pick_ref[f * entries : (f + 1) * entries, :] = jnp.dot(
            chooser, surface, preferred_element_type=jnp.float32
        )
    pick_ref[FA * entries :, :] = jnp.zeros((entries, R), jnp.float32)

    member = lax.rem(lax.broadcasted_iota(jnp.int32, (16, R), 0), 4)
    def chunk(n, carry):
        span = pl.ds(n * per_chunk, per_chunk)
        pltpu.make_async_copy(w_ref.at[:, span], w_vmem.at[:, span], w_sems.at[n]).wait()
        for step in range(per_chunk):
            g = n * per_chunk + step
            picked = pick_ref[pl.ds(g, 16, stride=quarter), :]
            rows = jnp.concatenate(
                [jnp.where(member < 2, picked, 0.0), jnp.where(member >= 2, picked, 0.0)], axis=1
            ).astype(jnp.bfloat16)
            block = jnp.concatenate(
                [
                    jnp.concatenate([w_vmem[0, g], w_vmem[2, g]], axis=1),
                    jnp.concatenate([w_vmem[1, g], w_vmem[3, g]], axis=1),
                ],
                axis=0,
            )
            res = lax.dot_general(
                rows, block, (((1,), (1,)), ((), ())), preferred_element_type=jnp.float32
            )
            part_ref[pl.ds(g, 16, stride=quarter), :] = jnp.where(member % 2 == 0, res[:, :R], res[:, R:])
        return carry

    lax.fori_loop(0, chunks, chunk, 0)

    slot = tile * CAP + rank
    slots = lax.broadcasted_iota(jnp.int32, (n_tile * CAP, entries), 0).astype(jnp.float32)
    placer = ones_where(slots == slot)
    edge_slots = lax.broadcasted_iota(jnp.int32, (3 * n_tile * EDGE_ROWS, entries), 0).astype(jnp.float32)
    edge_placer = ones_where(edge_slots == edge_slot)
    for f in range(FA):
        high, low = split_two(part_ref[f * entries : (f + 1) * entries, :])
        values = jnp.concatenate([high, low], axis=1)
        start = f * FIELD_ROWS
        own, edge = (
            both[:, :R] + both[:, R:]
            for both in (
                jnp.dot(matrix, values, preferred_element_type=jnp.float32) for matrix in (placer, edge_placer)
            )
        )
        for t in range(n_tile):
            out_ref[t, start : start + CAP, :] = own[t * CAP : (t + 1) * CAP]
            for n, (ref, at) in enumerate(((out_ref, start + CAP), (out_ref, MAIN_ROWS + f * EDGE_ROWS), (third_ref, f * EDGE_ROWS))):
                row = (n * n_tile + t) * EDGE_ROWS
                ref[t, at : at + EDGE_ROWS, :] = edge[row : row + EDGE_ROWS]


def remap(is_sea, place, source, tile, slot, x, weights, n_tile, sizes):
    entries = weights.shape[0]
    chunks = 4
    vmem = pl.BlockSpec(memory_space=pltpu.VMEM)
    hbm = pl.BlockSpec(memory_space=pltpu.HBM)
    return pl.pallas_call(
        functools.partial(remap_kernel, sizes, n_tile, chunks),
        out_shape=[
            jax.ShapeDtypeStruct((n_tile, rows, R), jnp.float32)
            for rows in (CHUNK_ROWS, FA * EDGE_ROWS)
        ],
        in_specs=[pl.BlockSpec(memory_space=pltpu.SMEM)] * 2 + [vmem, vmem, vmem, hbm, hbm],
        out_specs=[vmem] * 2,
        scratch_shapes=[
            pltpu.VMEM((4, entries // 4, R, R), jnp.bfloat16),
            pltpu.VMEM((FA * sizes[1], R), jnp.float32),
            pltpu.VMEM((4 * entries, R), jnp.float32),
            pltpu.VMEM((4 * entries, R), jnp.float32),
            pltpu.SemaphoreType.DMA((chunks,)),
            pltpu.SemaphoreType.DMA((FA,)),
        ],
        compiler_params=pltpu.CompilerParams(vmem_limit_bytes=LIMIT * MIB),
        cost_estimate=pl.CostEstimate(
            flops=2000 * entries * R * R, bytes_accessed=weights.size * 2, transcendentals=0
        ),
        name="remap",
    )(is_sea, place, source, tile, slot, x, weights.reshape(4, entries // 4, R, R))


def join_kernel(comp_ref, sent_ref, handed_ref, out_ref, sem):
    @pl.when(comp_ref[0] == 2)
    def _():
        copy = pltpu.make_async_copy(handed_ref, out_ref.at[:, pl.ds(MAIN_ROWS, FA * EDGE_ROWS)], sem)
        copy.start()
        copy.wait()


def join(comp, sent, handed):
    hbm = pl.BlockSpec(memory_space=pltpu.HBM)
    return pl.pallas_call(
        join_kernel,
        out_shape=jax.ShapeDtypeStruct(sent.shape, jnp.float32),
        in_specs=[pl.BlockSpec(memory_space=pltpu.SMEM), hbm, pl.BlockSpec(memory_space=pltpu.VMEM)],
        out_specs=hbm,
        input_output_aliases={1: 0},
        scratch_shapes=[pltpu.SemaphoreType.DMA(())],
        compiler_params=pltpu.CompilerParams(vmem_limit_bytes=LIMIT * MIB),
        cost_estimate=pl.CostEstimate(flops=0, bytes_accessed=0, transcendentals=0),
        name="join",
    )(comp, sent, handed)


def combine_kernel(sizes, comp_ref, recv_ref, first_ref, keep_ref, mine_ref, share_ref):
    atm_cols, sea_cols = sizes
    n_tile, per_group = recv_ref.shape[0], share_ref.shape[2]
    rows = 4 * per_group
    spots = lax.broadcasted_iota(jnp.int32, (rows, R), 0).astype(jnp.float32) + 1.0
    total = [jnp.zeros((rows, R), jnp.float32) for _ in range(FA)]
    for g in range(n_tile // 8):
        some = slice(g * 8, (g + 1) * 8)
        code = jnp.sum(recv_ref[some, FA * FIELD_ROWS, :], axis=0, keepdims=True)
        pick = ones_where(spots == code)
        for f in range(FA):
            start = f * FIELD_ROWS
            high, low = split_two(recv_ref[some, start : start + CAP, :].reshape(8 * CAP, R))
            both = jnp.dot(
                pick, jnp.concatenate([high, low], axis=1), preferred_element_type=jnp.float32
            )
            total[f] = total[f] + (both[:, :R] + both[:, R:])
    for f in range(FA):
        for c in range(4):
            share_ref[c, f] = total[f][c * per_group : (c + 1) * per_group]
    comp = comp_ref[0]
    mine_ref[...] = jnp.zeros_like(mine_ref)
    for f in range(FA):
        starts = (f * FIELD_ROWS + CAP, MAIN_ROWS + f * EDGE_ROWS)
        edge, extra = (jnp.sum(recv_ref[:, at : at + EDGE_ROWS, :], axis=0) for at in starts)

        def place(ref, cols, rows, f=f):
            ref[f, 0:HALO, :] = rows[:HALO]
            ref[f, HALO + cols : 2 * HALO + cols, :] = rows[HALO:]

        @pl.when(comp != 3)
        def _(place=place, edge=edge):
            place(share_ref.at[3], sea_cols, edge)

        @pl.when(comp == 2)
        def _(place=place, extra=extra):
            place(mine_ref, atm_cols, extra)

        @pl.when(comp == 3)
        def _(place=place, edge=edge, extra=extra):
            place(share_ref.at[0], atm_cols, edge)
            place(share_ref.at[1], atm_cols, extra)

    @pl.when(comp == 3)
    def _():
        first_ref[0] = share_ref[0]
        first_ref[1] = share_ref[2]
        keep_ref[...] = share_ref[1]

    @pl.when(comp != 3)
    def _():
        ocean = share_ref[3]
        first_ref[0] = jnp.where(comp == 1, 0.0, ocean)
        first_ref[1] = jnp.zeros_like(ocean)
        keep_ref[...] = jnp.where(comp == 1, ocean, 0.0)


def combine(comp, recv, sizes):
    vmem = pl.BlockSpec(memory_space=pltpu.VMEM)
    shape = (FA, sizes[1] + 2 * HALO, R)
    return pl.pallas_call(
        functools.partial(combine_kernel, sizes),
        out_shape=[jax.ShapeDtypeStruct(s, jnp.float32) for s in ((2,) + shape, shape, shape)],
        in_specs=[pl.BlockSpec(memory_space=pltpu.SMEM), vmem],
        out_specs=[vmem] * 3,
        scratch_shapes=[pltpu.VMEM((4,) + shape, jnp.float32)],
        compiler_params=pltpu.CompilerParams(vmem_limit_bytes=16 * MIB),
        name="combine",
    )(comp, recv)


def edges_kernel(sea_ref, x_atm_ref, x_sea_ref, mask_hbm, low_ref, high_ref, mask_ref, sems):
    mask_copy = pltpu.make_async_copy(mask_hbm, mask_ref, sems.at[2])
    mask_copy.start()
    for sea, x_ref in ((False, x_atm_ref), (True, x_sea_ref)):
        count, blocks = x_ref.shape[0], x_ref.shape[1]

        @pl.when((sea_ref[0] != 0) == sea)
        def _(sea=sea, x_ref=x_ref, count=count, blocks=blocks):
            copies = [
                pltpu.make_async_copy(x_ref.at[:, 0], low_ref.at[pl.ds(0, count)], sems.at[0]),
                pltpu.make_async_copy(x_ref.at[:, blocks - 1], high_ref.at[pl.ds(0, count)], sems.at[1]),
            ]
            for copy in copies:
                copy.start()
            mask_copy.wait()
            for ref, block in ((low_ref, 0), (high_ref, blocks - 1)):
                if count < FA * LA:
                    ref[count : FA * LA] = jnp.zeros((FA * LA - count, HALO, R), jnp.float32)
                ref[FA * LA : FA * LA + 1] = mask_ref[block : block + 1].astype(jnp.float32)
                ref[FA * LA + 1 :] = jnp.zeros((ref.shape[0] - FA * LA - 1, HALO, R), jnp.float32)
            for copy in copies:
                copy.wait()


def edge_columns(is_sea, state, mask, sizes):
    atm_cols, sea_cols = sizes
    hbm = pl.BlockSpec(memory_space=pltpu.HBM)
    vmem = pl.BlockSpec(memory_space=pltpu.VMEM)
    shape = jax.ShapeDtypeStruct((FA * LA + 2, HALO, R), jnp.float32)
    return pl.pallas_call(
        edges_kernel,
        out_shape=[shape, shape],
        in_specs=[pl.BlockSpec(memory_space=pltpu.SMEM), hbm, hbm, hbm],
        out_specs=[vmem, vmem],
        scratch_shapes=[pltpu.VMEM((sea_cols // HALO, HALO, R), jnp.int32), pltpu.SemaphoreType.DMA((3,))],
        compiler_params=pltpu.CompilerParams(vmem_limit_bytes=LIMIT * MIB),
        name="edges",
    )(
        is_sea,
        state.reshape(FA * LA, atm_cols // HALO, HALO, R),
        state.reshape(FO * LO, sea_cols // HALO, HALO, R),
        mask.reshape(sea_cols // HALO, HALO, R),
    )


def filtered_twice(cols, nu, column, mask, operator, lhs_ref, mid_ref, store):
    def middle(k):
        return mid_ref[(k + 2) * 16 : (k + 3) * 16, :]

    def keep(k, plane):
        mid_ref[(k + 2) * 16 : (k + 3) * 16, :] = plane

    filter_planes(column, -2, cols + 2, nu, mask, operator, lhs_ref.at[0], keep)
    filter_planes(middle, 0, cols, nu, mask, operator, lhs_ref.at[1], store)


def dynamics_part(
    fields, levels, cols, surface, side, nu, x_ref, left_ref, right_ref, matrix_ref, masked, mask_ref, out_ref, column_ref,
    mask_vmem, x_vmem, out_vmem, op_ref, y_vmem, lhs_ref, mid_ref, in_sems, out_sems
):
    rows = levels * cols

    def read(f):
        span = pl.ds(pl.multiple_of(f * rows, 8), rows)
        return pltpu.make_async_copy(x_ref.at[span], x_vmem.at[span], in_sems.at[f])

    def write(f):
        span = pl.ds(pl.multiple_of(f * rows, 8), rows)
        return pltpu.make_async_copy(out_vmem.at[span], out_ref.at[span], out_sems.at[f])

    read(0).start()
    op_ref[...] = row_operator()
    spare = FA * LA * HALO
    mask_vmem[0:HALO, :] = jnp.zeros((HALO, R), jnp.float32)
    mask_vmem[HALO : 2 * HALO, :] = left_ref[spare : spare + HALO, :]
    mask_vmem[8 : 8 + cols, :] = mask_ref[:cols].astype(jnp.float32)
    mask_vmem[8 + cols : 8 + HALO + cols, :] = right_ref[spare : spare + HALO, :]
    tail = mask_vmem.shape[0] - 8 - HALO - cols
    mask_vmem[8 + HALO + cols :, :] = jnp.zeros((tail, R), jnp.float32)
    mask = None
    if masked:
        mask = lambda k: jnp.broadcast_to(mask_vmem[k + 8 : k + 9, :], (16, R))

    def field(f, carry):
        squared = jnp.dot(
            matrix_ref[f], matrix_ref[f], precision=lax.Precision.HIGHEST, preferred_element_type=jnp.float32
        )
        column_ref[pl.ds(pl.multiple_of(f * levels, 8), levels), :] = jnp.broadcast_to(
            squared[:, surface : surface + 1], (levels, R)
        )
        high, low = split_two(squared)
        stacked = jnp.concatenate(
            [jnp.concatenate([high, high], axis=1), jnp.concatenate([low, jnp.zeros_like(low)], axis=1)], axis=0
        )
        read(f).wait()

        @pl.when(f + 1 < fields)
        def _():
            read(f + 1).start()

        def filter_rows(i, slot):
            first = f * levels + i * 16
            spot = pl.multiple_of(i * 16, 16)

            def column(k):
                if k < 0:
                    return left_ref[pl.ds(first * HALO + k + HALO, 16, stride=HALO), :]
                if k >= cols:
                    return right_ref[pl.ds(first * HALO + k - cols, 16, stride=HALO), :]
                return x_vmem[pl.ds(first * cols + k, 16, stride=cols), :]

            def store(k, plane):
                high, low = split_two(plane)
                y_vmem[pl.ds(spot, 16), k * R : (k + 1) * R] = high
                y_vmem[pl.ds(levels + spot, 16), k * R : (k + 1) * R] = low

            filtered_twice(cols, nu, column, mask, op_ref[...], lhs_ref.at[slot], mid_ref.at[slot], store)

        def filter_some(n, carry):
            for slot in range(side):
                filter_rows(n * side + slot, slot)
            return carry

        lax.fori_loop(0, levels // 16 // side, filter_some, 0)

        for pair in range(cols // 2):
            both = jnp.dot(
                stacked,
                y_vmem[: 2 * levels, 2 * pair * R : 2 * (pair + 1) * R],
                preferred_element_type=jnp.float32,
            )
            mixed = both[:levels] + both[levels:]
            for h in range(2):
                out_vmem[pl.ds(f * rows + 2 * pair + h, levels, stride=cols), :] = mixed[:, h * R : (h + 1) * R]
        write(f).start()
        return carry

    lax.fori_loop(0, fields, field, 0)
    for f in range(fields):
        write(f).wait()


def dynamics_kernel(
    sizes, sea_ref, x_ref, left_ref, right_ref, atm_ref, ocean_ref, mask_ref, *rest
):
    atm_cols, sea_cols = sizes

    @pl.when(sea_ref[0] == 0)
    def _():
        dynamics_part(
            FA, LA, atm_cols, LA - 1, SIDE[0], NU_ATMOS, x_ref, left_ref, right_ref, atm_ref, False, mask_ref, *rest
        )

    @pl.when(sea_ref[0] != 0)
    def _():
        dynamics_part(
            FO, LO, sea_cols, 0, SIDE[1], NU_OCEAN, x_ref, left_ref, right_ref, ocean_ref, True, mask_ref, *rest
        )


def dynamics(is_sea, x, left, right, atm_mixing, ocean_mixing, mask, sizes):
    vmem = pl.BlockSpec(memory_space=pltpu.VMEM)
    hbm = pl.BlockSpec(memory_space=pltpu.HBM)
    rows = x.shape[0]
    widest = max(sizes)
    return pl.pallas_call(
        functools.partial(dynamics_kernel, sizes),
        out_shape=[
            jax.ShapeDtypeStruct((rows, R), jnp.float32),
            jax.ShapeDtypeStruct((FA * LA, R), jnp.float32),
            jax.ShapeDtypeStruct((widest + 16, R), jnp.float32),
        ],
        in_specs=[pl.BlockSpec(memory_space=pltpu.SMEM), hbm] + [vmem] * 5,
        out_specs=[hbm, vmem, vmem],
        scratch_shapes=[
            pltpu.VMEM((rows, R), jnp.float32),
            pltpu.VMEM((rows, R), jnp.float32),
            pltpu.VMEM((2 * R, 2 * R), jnp.bfloat16),
            pltpu.VMEM((2 * LA, widest * R), jnp.bfloat16),
            pltpu.VMEM((max(SIDE), 2, (widest + 6) * 16, 2 * R), jnp.bfloat16),
            pltpu.VMEM((max(SIDE), (widest + 4) * 16, R), jnp.float32),
            pltpu.SemaphoreType.DMA((FO,)),
            pltpu.SemaphoreType.DMA((FO,)),
        ],
        compiler_params=pltpu.CompilerParams(vmem_limit_bytes=LIMIT * MIB),
        cost_estimate=pl.CostEstimate(
            flops=100 * rows * R * R, bytes_accessed=16 * rows * R, transcendentals=0
        ),
        name="dynamics",
    )(is_sea, x, left, right, atm_mixing, ocean_mixing, mask)


def lane_edges(rows):
    lane = lax.broadcasted_iota(jnp.int32, (rows, R), 1)
    return lane == 0, lane == R - 1


def lap(before, middle, after, edges):
    first, last = edges
    down = jnp.where(first, 0.0, pltpu.roll(middle, 1, 1))
    up = jnp.where(last, 0.0, pltpu.roll(middle, R - 1, 1))
    return (before + after) + (down + up) - 4.0 * middle


def filter_forcing(cols, nu, forcing_of, masked, mask_ref, work_ref, g_ref):
    lo, hi, rows = 8, 8 + cols, cols + 16
    edges = lane_edges(rows)
    mask = mask_ref[0:rows, :]

    def along(v):
        return lap(pltpu.roll(v, 1, 0), v, pltpu.roll(v, rows - 1, 0), edges)

    for f in range(FA):
        work_ref[0:rows, :] = jnp.zeros((rows, R), jnp.float32)
        work_ref[lo - HALO : hi + HALO, :] = COUPLE_RATE * forcing_of(f)
        value = work_ref[0:rows, :] * mask
        for _ in range(2):
            value = value - nu * along(along(value))
            if masked:
                value = value * mask
        g_ref[f, :cols] = value[lo:hi]


def update_part(
    cols, levels, fields, pieces, masked, nu, comp_ref, column_ref, part_ref, first_ref, second_ref, mine_ref, mask_ref, out_ref,
    work_ref, g_ref, stage_ref, out_sems
):
    per_piece = fields * levels // pieces
    rows = per_piece * cols

    def write(p):
        span = pl.ds(pl.multiple_of(p * rows, 8), rows)
        return pltpu.make_async_copy(stage_ref.at[span], out_ref.at[span], out_sems.at[p])

    wide = cols + 2 * HALO

    def forcing_of(f):
        if fields == FO:
            return first_ref[0, f, :wide] + second_ref[f, :wide]
        own = first_ref[1, f, :wide] + mine_ref[f, :wide]
        return jnp.where(comp_ref[0] == 2, own, 0.0) + second_ref[f, :wide]

    filter_forcing(cols, nu, forcing_of, masked, mask_ref, work_ref, g_ref)

    def piece(p, carry):
        field = p * per_piece // levels

        @pl.when(field < FA)
        def _():
            pushed = [g_ref[field, v * 8 : v * 8 + 8, :] for v in range(cols // 8)]

            def group(q, carry):
                number = p * per_piece + q
                factor = jnp.broadcast_to(column_ref[pl.ds(number, 1), :], (8, R))
                for v in range(cols // 8):
                    span = pl.ds(pl.multiple_of(number * cols + v * 8, 8), 8)
                    stage_ref[span, :] = part_ref[span, :] + factor * pushed[v]
                return carry

            lax.fori_loop(0, per_piece, group, 0, unroll=8)

        @pl.when(field >= FA)
        def _():
            span = pl.ds(pl.multiple_of(p * rows, 8), rows)
            stage_ref[span, :] = part_ref[span, :]

        write(p).start()
        return carry

    lax.fori_loop(0, pieces, piece, 0)
    for p in range(pieces):
        write(p).wait()


def fetch_kernel(part_ref, after_ref, out_ref, sems):
    rows = part_ref.shape[0] // 8
    copies = []
    for p in range(8):
        span = pl.ds(p * rows, rows)
        copies.append(pltpu.make_async_copy(part_ref.at[span], out_ref.at[span], sems.at[p]))
        copies[-1].start()
    for copy in copies:
        copy.wait()


def fetch(part, after):
    vmem = pl.BlockSpec(memory_space=pltpu.VMEM)
    hbm = pl.BlockSpec(memory_space=pltpu.HBM)
    return pl.pallas_call(
        fetch_kernel,
        out_shape=pltpu.VMEM(part.shape, jnp.float32),
        in_specs=[hbm, hbm],
        out_specs=vmem,
        scratch_shapes=[pltpu.SemaphoreType.DMA((8,))],
        compiler_params=pltpu.CompilerParams(vmem_limit_bytes=40 * MIB),
        cost_estimate=pl.CostEstimate(flops=0, bytes_accessed=4 * part.size, transcendentals=0),
        name="fetch",
    )(part, after)


def update_kernel(sizes, comp_ref, *rest):
    atm_cols, sea_cols = sizes

    @pl.when(comp_ref[0] != 3)
    def _():
        update_part(atm_cols, LA, FA, 4 * FA, False, NU_ATMOS, comp_ref, *rest)

    @pl.when(comp_ref[0] == 3)
    def _():
        update_part(sea_cols, LO, FO, 2 * FO, True, NU_OCEAN, comp_ref, *rest)


def update(comp, column, part, first, second, mine, mask, sizes):
    vmem = pl.BlockSpec(memory_space=pltpu.VMEM)
    hbm = pl.BlockSpec(memory_space=pltpu.HBM)
    rows = part.shape[0]
    return pl.pallas_call(
        functools.partial(update_kernel, sizes),
        out_shape=jax.ShapeDtypeStruct((rows, R), jnp.float32),
        in_specs=[pl.BlockSpec(memory_space=pltpu.SMEM)] + [vmem] * 6,
        out_specs=hbm,
        scratch_shapes=[
            pltpu.VMEM((max(sizes) + 16, R), jnp.float32),
            pltpu.VMEM((FA, max(sizes), R), jnp.float32),
            pltpu.VMEM((rows, R), jnp.float32),
            pltpu.SemaphoreType.DMA((4 * FA,)),
        ],
        compiler_params=pltpu.CompilerParams(vmem_limit_bytes=40 * MIB),
        cost_estimate=pl.CostEstimate(
            flops=2 * rows * R, bytes_accessed=8 * rows * R, transcendentals=0
        ),
        name="update",
    )(comp, column, part, first, second, mine, mask)


def local(
    fields, atm_mixing, ocean_mixing, sea_mask, source_slot, target_tile, target_slot, remap_blocks
):
    n_comp = lax.axis_size("comp")
    n_tile = lax.axis_size("tile")
    is_sea = lax.axis_index("comp") == n_comp - 1
    sea_cols = sea_mask.shape[2]
    atm_cols = sea_cols * 5 // 6
    sizes = (atm_cols, sea_cols)
    sea_flag = is_sea.astype(jnp.int32).reshape(1)
    mask = sea_mask[0, 0]
    state = fields[0, 0]
    tiles = target_tile[0, 0, :, 0]
    weights = remap_blocks[0, 0]
    forward = [(i, (i + 1) % n_tile) for i in range(n_tile)]
    backward = [(b, a) for a, b in forward]

    low_edge, high_edge = edge_columns(sea_flag, state, mask, sizes)
    low_edge, high_edge, tiles = lax.optimization_barrier((low_edge, high_edge, tiles))
    left = lax.ppermute(high_edge, "tile", forward)
    right = lax.ppermute(low_edge, "tile", backward)

    sent, third = remap(
        sea_flag,
        lax.axis_index("tile").reshape(1),
        source_slot.reshape(1, -1),
        tiles.reshape(1, -1),
        target_slot.reshape(1, -1),
        state.reshape(-1, R),
        weights,
        n_tile,
        sizes,
    )
    comp = lax.axis_index("comp")
    handed = lax.ppermute(third, "comp", [(3, 2)])
    comp_flag = comp.reshape(1)
    sent = join(comp_flag, sent, handed)
    received = lax.all_to_all(sent, "tile", split_axis=0, concat_axis=0, tiled=True)

    x = state.reshape(-1, R)
    flat_left = left.reshape(-1, R)
    flat_right = right.reshape(-1, R)
    part, column, wide_mask = dynamics(sea_flag, x, flat_left, flat_right, atm_mixing, ocean_mixing, mask, sizes)

    received, part = lax.optimization_barrier((received, part))
    first, keep, mine = combine(comp_flag, received, sizes)
    other_core = lax.ppermute(first, "comp", [(0, 1), (1, 0), (2, 3), (3, 2)])
    onward = keep + jnp.where(comp == 3, 0.0, other_core[0])
    other_chip = lax.ppermute(onward, "comp", [(0, 2), (2, 0), (1, 3), (3, 1)])
    part = fetch(part, onward)
    done = update(comp_flag, column, part, other_core, other_chip, mine, wide_mask, sizes)
    return done.reshape(1, 1, -1)


def solution(mesh):
    in_specs = (
        P("comp", "tile", None),
        P(),
        P(),
        P("comp", "tile", None, None),
        P("comp", "tile", None),
        P("comp", "tile", None, None),
        P("comp", "tile", None),
        P("comp", "tile", None, None, None),
    )
    out_specs = P("comp", "tile", None)
    return jax.shard_map(local, mesh=mesh, in_specs=in_specs, out_specs=out_specs, check_vma=False)
```

```python
import functools

import jax
import jax.numpy as jnp
from jax import lax
from jax.experimental import pallas as pl
from jax.experimental.pallas import tpu as pltpu
from jax.sharding import PartitionSpec as P

FA = 3
FO = 4
LA = 128
LO = 80
R = 128
CAP = 16

COUPLE_RATE = 0.1
NU_ATMOS = 0.02
NU_OCEAN = 0.015

HALO = 4
EDGE_ROWS = 2 * HALO
FIELD_ROWS = CAP + EDGE_ROWS
MAIN_ROWS = FA * FIELD_ROWS + 8
CHUNK_ROWS = MAIN_ROWS + FA * EDGE_ROWS
MIB = 1 << 20
LIMIT = 52
SIDE = (8, 5)


def split_two(value):
    high = value.astype(jnp.bfloat16)
    return high, (value - high.astype(jnp.float32)).astype(jnp.bfloat16)


def row_operator():
    row = lax.broadcasted_iota(jnp.int32, (R, R), 0)
    lane = lax.broadcasted_iota(jnp.int32, (R, R), 1)
    apart = jnp.abs(row - lane)
    u = jnp.where(apart == 0, -4.0, jnp.where(apart == 1, 1.0, 0.0))
    ends = jnp.where((row == 0) | (row == R - 1), 1.0, 0.0)
    squared = jnp.where(apart == 1, -8.0, jnp.where(apart == 2, 1.0, 0.0))
    squared = jnp.where(apart == 0, 20.0 - ends, squared)
    both = jnp.concatenate([2.0 * u, squared], axis=1).astype(jnp.bfloat16)
    return jnp.concatenate([both, both], axis=0)


def apply_filter(value, column_sums, row_parts, nu):
    return value - nu * (column_sums + row_parts)


def filter_planes(column, first, last, nu, mask, operator, lhs_ref, emit):
    rows = 16
    for k in range(first - 1, last + 1):
        spot = (k - first + 1) * rows
        high, low = split_two(column(k))
        lhs_ref[spot : spot + rows, :R] = high
        lhs_ref[spot : spot + rows, R:] = low
    both = jnp.dot(
        lhs_ref[: (last - first + 2) * rows], operator, preferred_element_type=jnp.float32
    )

    def part(k, half):
        spot = (k - first + 1) * rows
        return both[spot : spot + rows, half * R : (half + 1) * R]

    for k in range(first, last):
        column_sums = column(k - 2) + column(k + 2)
        row_parts = (part(k - 1, 0) + part(k + 1, 0)) + part(k, 1)
        plane = apply_filter(column(k), column_sums, row_parts, nu)
        if mask is not None:
            plane = plane * mask(k)
        emit(k, plane)


def surface_copies(sizes, sea, x_ref, surf_ref, sems):
    atm_cols, sea_cols = sizes
    if sea:
        cols, starts = sea_cols, [f * LO * sea_cols for f in range(FA)]
    else:
        cols, starts = atm_cols, [(f * LA + LA - 1) * atm_cols for f in range(FA)]
    return [
        pltpu.make_async_copy(
            x_ref.at[pl.ds(start, cols)], surf_ref.at[pl.ds(f * sea_cols, cols)], sems.at[f]
        )
        for f, start in enumerate(starts)
    ]


def small_mod(value, modulus, limit):
    for step in range(modulus, limit, modulus):
        value = jnp.where(value >= modulus, value - modulus, value)
    return value


def as_column(row):
    n = row.shape[1]
    diagonal = lax.broadcasted_iota(jnp.int32, (n, n), 0) == lax.broadcasted_iota(jnp.int32, (n, n), 1)
    return jnp.sum(jnp.where(diagonal, row, 0.0), axis=1, keepdims=True)


def ones_where(condition):
    return jnp.where(condition, 1.0, 0.0).astype(jnp.bfloat16)


def remap_kernel(
    sizes, n_tile, chunks, sea_ref, place_ref, source_ref, tile_ref, slot_ref, x_ref, w_ref, out_ref, third_ref, w_vmem, surf_ref, pick_ref, part_ref, w_sems, x_sems
):
    atm_cols, sea_cols = sizes
    entries = source_ref.shape[1]
    quarter = entries // 4
    per_chunk = quarter // chunks
    code_limit = 5 * sea_cols
    copies = [
        pltpu.make_async_copy(
            w_ref.at[:, pl.ds(n * per_chunk, per_chunk)], w_vmem.at[:, pl.ds(n * per_chunk, per_chunk)], w_sems.at[n]
        )
        for n in range(chunks)
    ]
    is_sea = sea_ref[0] != 0
    for sea in (False, True):

        @pl.when(is_sea == sea)
        def _(sea=sea):
            for copy in surface_copies(sizes, sea, x_ref, surf_ref, x_sems):
                copy.start()

    for copy in copies:
        copy.start()

    tile = tile_ref[...].astype(jnp.float32)
    tile_column = as_column(tile)
    earlier = lax.broadcasted_iota(jnp.int32, (entries, entries), 0) < lax.broadcasted_iota(
        jnp.int32, (entries, entries), 1
    )
    rank = jnp.sum(jnp.where((tile_column == tile) & earlier, 1.0, 0.0), axis=0, keepdims=True)
    code = slot_ref[...]
    for_atm = small_mod(code, 3 * atm_cols, code_limit)
    for_atm_block = small_mod(for_atm, atm_cols, 3 * atm_cols)
    for_atm_group = jnp.where(for_atm >= atm_cols, 1, 0) + jnp.where(for_atm >= 2 * atm_cols, 1, 0)
    for_sea_block = small_mod(code, sea_cols, code_limit)
    window = sea_cols + 2 * HALO
    group = jnp.where(is_sea, for_atm_group, 3)
    block = jnp.where(is_sea, for_atm_block, for_sea_block)
    dest = (group * window + block + HALO + 1).astype(jnp.float32)
    lane = rank + (CAP * lax.rem(place_ref[0], R // CAP)).astype(jnp.float32)
    spots = lax.broadcasted_iota(jnp.int32, (R, entries), 0).astype(jnp.float32)
    marks = jnp.where(spots == lane, dest, 0.0).astype(jnp.bfloat16)
    tiles = lax.broadcasted_iota(jnp.int32, (n_tile, entries), 0).astype(jnp.float32)
    codes = lax.dot_general(
        ones_where(tiles == tile), marks, (((1,), (1,)), ((), ())), preferred_element_type=jnp.float32
    )
    tile_number = tile_ref[...]
    high_start = jnp.where(is_sea, atm_cols, sea_cols) - HALO
    edge_tile = jnp.where(block < HALO, tile_number + n_tile - 1, tile_number + 1)
    edge_tile = jnp.where(edge_tile >= n_tile, edge_tile - n_tile, edge_tile)
    edge_row = jnp.where(block < HALO, block + HALO, block - high_start)
    edge_row = (jnp.where(is_sea, group, 0) * n_tile + edge_tile) * EDGE_ROWS + edge_row
    on_edge = (block < HALO) | (block >= high_start)
    edge_slot = jnp.where(on_edge, edge_row, -1).astype(jnp.float32)
    tail = MAIN_ROWS - FA * FIELD_ROWS
    for t in range(n_tile):
        out_ref[t, FA * FIELD_ROWS : MAIN_ROWS, :] = jnp.concatenate(
            [codes[t : t + 1], jnp.zeros((tail - 1, R), jnp.float32)], axis=0
        )

    source = source_ref[...]
    source = jnp.where(
        is_sea, small_mod(source, sea_cols, code_limit), small_mod(source, atm_cols, code_limit)
    )
    source_column = as_column(source.astype(jnp.float32))
    columns = lax.broadcasted_iota(jnp.int32, (entries, sea_cols), 1).astype(jnp.float32)
    chooser = ones_where(columns == source_column)
    for sea in (False, True):

        @pl.when(is_sea == sea)
        def _(sea=sea):
            for copy in surface_copies(sizes, sea, x_ref, surf_ref, x_sems):
                copy.wait()
            if not sea:
                for f in range(FA):
                    surf_ref[f * sea_cols + atm_cols : (f + 1) * sea_cols, :] = jnp.zeros(
                        (sea_cols - atm_cols, R), jnp.float32
                    )

    for f in range(FA):
        surface = surf_ref[f * sea_cols : (f + 1) * sea_cols, :].astype(jnp.bfloat16)
        pick_ref[f * entries : (f + 1) * entries, :] = jnp.dot(
            chooser, surface, preferred_element_type=jnp.float32
        )
    pick_ref[FA * entries :, :] = jnp.zeros((entries, R), jnp.float32)

    member = lax.rem(lax.broadcasted_iota(jnp.int32, (16, R), 0), 4)
    def chunk(n, carry):
        span = pl.ds(n * per_chunk, per_chunk)
        pltpu.make_async_copy(w_ref.at[:, span], w_vmem.at[:, span], w_sems.at[n]).wait()
        for step in range(per_chunk):
            g = n * per_chunk + step
            picked = pick_ref[pl.ds(g, 16, stride=quarter), :]
            rows = jnp.concatenate(
                [jnp.where(member < 2, picked, 0.0), jnp.where(member >= 2, picked, 0.0)], axis=1
            ).astype(jnp.bfloat16)
            block = jnp.concatenate(
                [
                    jnp.concatenate([w_vmem[0, g], w_vmem[2, g]], axis=1),
                    jnp.concatenate([w_vmem[1, g], w_vmem[3, g]], axis=1),
                ],
                axis=0,
            )
            res = lax.dot_general(
                rows, block, (((1,), (1,)), ((), ())), preferred_element_type=jnp.float32
            )
            part_ref[pl.ds(g, 16, stride=quarter), :] = jnp.where(member % 2 == 0, res[:, :R], res[:, R:])
        return carry

    lax.fori_loop(0, chunks, chunk, 0)

    slot = tile * CAP + rank
    slots = lax.broadcasted_iota(jnp.int32, (n_tile * CAP, entries), 0).astype(jnp.float32)
    placer = ones_where(slots == slot)
    edge_slots = lax.broadcasted_iota(jnp.int32, (3 * n_tile * EDGE_ROWS, entries), 0).astype(jnp.float32)
    edge_placer = ones_where(edge_slots == edge_slot)
    for f in range(FA):
        high, low = split_two(part_ref[f * entries : (f + 1) * entries, :])
        values = jnp.concatenate([high, low], axis=1)
        start = f * FIELD_ROWS
        own, edge = (
            both[:, :R] + both[:, R:]
            for both in (
                jnp.dot(matrix, values, preferred_element_type=jnp.float32) for matrix in (placer, edge_placer)
            )
        )
        for t in range(n_tile):
            out_ref[t, start : start + CAP, :] = own[t * CAP : (t + 1) * CAP]
            for n, (ref, at) in enumerate(((out_ref, start + CAP), (out_ref, MAIN_ROWS + f * EDGE_ROWS), (third_ref, f * EDGE_ROWS))):
                row = (n * n_tile + t) * EDGE_ROWS
                ref[t, at : at + EDGE_ROWS, :] = edge[row : row + EDGE_ROWS]


def remap(is_sea, place, source, tile, slot, x, weights, n_tile, sizes):
    entries = weights.shape[0]
    chunks = 4
    vmem = pl.BlockSpec(memory_space=pltpu.VMEM)
    hbm = pl.BlockSpec(memory_space=pltpu.HBM)
    return pl.pallas_call(
        functools.partial(remap_kernel, sizes, n_tile, chunks),
        out_shape=[
            jax.ShapeDtypeStruct((n_tile, rows, R), jnp.float32)
            for rows in (CHUNK_ROWS, FA * EDGE_ROWS)
        ],
        in_specs=[pl.BlockSpec(memory_space=pltpu.SMEM)] * 2 + [vmem, vmem, vmem, hbm, hbm],
        out_specs=[vmem] * 2,
        scratch_shapes=[
            pltpu.VMEM((4, entries // 4, R, R), jnp.bfloat16),
            pltpu.VMEM((FA * sizes[1], R), jnp.float32),
            pltpu.VMEM((4 * entries, R), jnp.float32),
            pltpu.VMEM((4 * entries, R), jnp.float32),
            pltpu.SemaphoreType.DMA((chunks,)),
            pltpu.SemaphoreType.DMA((FA,)),
        ],
        compiler_params=pltpu.CompilerParams(vmem_limit_bytes=LIMIT * MIB),
        cost_estimate=pl.CostEstimate(
            flops=2000 * entries * R * R, bytes_accessed=weights.size * 2, transcendentals=0
        ),
        name="remap",
    )(is_sea, place, source, tile, slot, x, weights.reshape(4, entries // 4, R, R))


def join_kernel(comp_ref, sent_ref, handed_ref, out_ref, sem):
    @pl.when(comp_ref[0] == 2)
    def _():
        copy = pltpu.make_async_copy(handed_ref, out_ref.at[:, pl.ds(MAIN_ROWS, FA * EDGE_ROWS)], sem)
        copy.start()
        copy.wait()


def join(comp, sent, handed):
    hbm = pl.BlockSpec(memory_space=pltpu.HBM)
    return pl.pallas_call(
        join_kernel,
        out_shape=jax.ShapeDtypeStruct(sent.shape, jnp.float32),
        in_specs=[pl.BlockSpec(memory_space=pltpu.SMEM), hbm, pl.BlockSpec(memory_space=pltpu.VMEM)],
        out_specs=hbm,
        input_output_aliases={1: 0},
        scratch_shapes=[pltpu.SemaphoreType.DMA(())],
        compiler_params=pltpu.CompilerParams(vmem_limit_bytes=LIMIT * MIB),
        cost_estimate=pl.CostEstimate(flops=0, bytes_accessed=0, transcendentals=0),
        name="join",
    )(comp, sent, handed)


def combine_kernel(sizes, comp_ref, recv_ref, first_ref, keep_ref, mine_ref, share_ref):
    atm_cols, sea_cols = sizes
    n_tile, per_group = recv_ref.shape[0], share_ref.shape[2]
    rows = 4 * per_group
    spots = lax.broadcasted_iota(jnp.int32, (rows, R), 0).astype(jnp.float32) + 1.0
    total = [jnp.zeros((rows, R), jnp.float32) for _ in range(FA)]
    for g in range(n_tile // 8):
        some = slice(g * 8, (g + 1) * 8)
        code = jnp.sum(recv_ref[some, FA * FIELD_ROWS, :], axis=0, keepdims=True)
        pick = ones_where(spots == code)
        for f in range(FA):
            start = f * FIELD_ROWS
            high, low = split_two(recv_ref[some, start : start + CAP, :].reshape(8 * CAP, R))
            both = jnp.dot(
                pick, jnp.concatenate([high, low], axis=1), preferred_element_type=jnp.float32
            )
            total[f] = total[f] + (both[:, :R] + both[:, R:])
    for f in range(FA):
        for c in range(4):
            share_ref[c, f] = total[f][c * per_group : (c + 1) * per_group]
    comp = comp_ref[0]
    mine_ref[...] = jnp.zeros_like(mine_ref)
    for f in range(FA):
        starts = (f * FIELD_ROWS + CAP, MAIN_ROWS + f * EDGE_ROWS)
        edge, extra = (jnp.sum(recv_ref[:, at : at + EDGE_ROWS, :], axis=0) for at in starts)

        def place(ref, cols, rows, f=f):
            ref[f, 0:HALO, :] = rows[:HALO]
            ref[f, HALO + cols : 2 * HALO + cols, :] = rows[HALO:]

        @pl.when(comp != 3)
        def _(place=place, edge=edge):
            place(share_ref.at[3], sea_cols, edge)

        @pl.when(comp == 2)
        def _(place=place, extra=extra):
            place(mine_ref, atm_cols, extra)

        @pl.when(comp == 3)
        def _(place=place, edge=edge, extra=extra):
            place(share_ref.at[0], atm_cols, edge)
            place(share_ref.at[1], atm_cols, extra)

    @pl.when(comp == 3)
    def _():
        first_ref[0] = share_ref[0]
        first_ref[1] = share_ref[2]
        keep_ref[...] = share_ref[1]

    @pl.when(comp != 3)
    def _():
        ocean = share_ref[3]
        first_ref[0] = jnp.where(comp == 1, 0.0, ocean)
        first_ref[1] = jnp.zeros_like(ocean)
        keep_ref[...] = jnp.where(comp == 1, ocean, 0.0)


def combine(comp, recv, sizes):
    vmem = pl.BlockSpec(memory_space=pltpu.VMEM)
    shape = (FA, sizes[1] + 2 * HALO, R)
    return pl.pallas_call(
        functools.partial(combine_kernel, sizes),
        out_shape=[jax.ShapeDtypeStruct(s, jnp.float32) for s in ((2,) + shape, shape, shape)],
        in_specs=[pl.BlockSpec(memory_space=pltpu.SMEM), vmem],
        out_specs=[vmem] * 3,
        scratch_shapes=[pltpu.VMEM((4,) + shape, jnp.float32)],
        compiler_params=pltpu.CompilerParams(vmem_limit_bytes=16 * MIB),
        name="combine",
    )(comp, recv)


def edges_kernel(sea_ref, x_atm_ref, x_sea_ref, mask_hbm, low_ref, high_ref, mask_ref, sems):
    mask_copy = pltpu.make_async_copy(mask_hbm, mask_ref, sems.at[2])
    mask_copy.start()
    for sea, x_ref in ((False, x_atm_ref), (True, x_sea_ref)):
        count, blocks = x_ref.shape[0], x_ref.shape[1]

        @pl.when((sea_ref[0] != 0) == sea)
        def _(sea=sea, x_ref=x_ref, count=count, blocks=blocks):
            copies = [
                pltpu.make_async_copy(x_ref.at[:, 0], low_ref.at[pl.ds(0, count)], sems.at[0]),
                pltpu.make_async_copy(x_ref.at[:, blocks - 1], high_ref.at[pl.ds(0, count)], sems.at[1]),
            ]
            for copy in copies:
                copy.start()
            mask_copy.wait()
            for ref, block in ((low_ref, 0), (high_ref, blocks - 1)):
                if count < FA * LA:
                    ref[count : FA * LA] = jnp.zeros((FA * LA - count, HALO, R), jnp.float32)
                ref[FA * LA : FA * LA + 1] = mask_ref[block : block + 1].astype(jnp.float32)
                ref[FA * LA + 1 :] = jnp.zeros((ref.shape[0] - FA * LA - 1, HALO, R), jnp.float32)
            for copy in copies:
                copy.wait()


def edge_columns(is_sea, state, mask, sizes):
    atm_cols, sea_cols = sizes
    hbm = pl.BlockSpec(memory_space=pltpu.HBM)
    vmem = pl.BlockSpec(memory_space=pltpu.VMEM)
    shape = jax.ShapeDtypeStruct((FA * LA + 2, HALO, R), jnp.float32)
    return pl.pallas_call(
        edges_kernel,
        out_shape=[shape, shape],
        in_specs=[pl.BlockSpec(memory_space=pltpu.SMEM), hbm, hbm, hbm],
        out_specs=[vmem, vmem],
        scratch_shapes=[pltpu.VMEM((sea_cols // HALO, HALO, R), jnp.int32), pltpu.SemaphoreType.DMA((3,))],
        compiler_params=pltpu.CompilerParams(vmem_limit_bytes=LIMIT * MIB),
        name="edges",
    )(
        is_sea,
        state.reshape(FA * LA, atm_cols // HALO, HALO, R),
        state.reshape(FO * LO, sea_cols // HALO, HALO, R),
        mask.reshape(sea_cols // HALO, HALO, R),
    )


def filtered_twice(cols, nu, column, mask, operator, lhs_ref, mid_ref, store):
    def middle(k):
        return mid_ref[(k + 2) * 16 : (k + 3) * 16, :]

    def keep(k, plane):
        mid_ref[(k + 2) * 16 : (k + 3) * 16, :] = plane

    filter_planes(column, -2, cols + 2, nu, mask, operator, lhs_ref.at[0], keep)
    filter_planes(middle, 0, cols, nu, mask, operator, lhs_ref.at[1], store)


def dynamics_part(
    fields, levels, cols, surface, side, nu, x_ref, left_ref, right_ref, matrix_ref, masked, mask_ref, out_ref, column_ref,
    mask_vmem, x_vmem, out_vmem, op_ref, y_vmem, lhs_ref, mid_ref, in_sems, out_sems
):
    rows = levels * cols

    def read(f):
        span = pl.ds(pl.multiple_of(f * rows, 8), rows)
        return pltpu.make_async_copy(x_ref.at[span], x_vmem.at[span], in_sems.at[f])

    def write(f):
        span = pl.ds(pl.multiple_of(f * rows, 8), rows)
        return pltpu.make_async_copy(out_vmem.at[span], out_ref.at[span], out_sems.at[f])

    read(0).start()
    op_ref[...] = row_operator()
    spare = FA * LA * HALO
    mask_vmem[0:HALO, :] = jnp.zeros((HALO, R), jnp.float32)
    mask_vmem[HALO : 2 * HALO, :] = left_ref[spare : spare + HALO, :]
    mask_vmem[8 : 8 + cols, :] = mask_ref[:cols].astype(jnp.float32)
    mask_vmem[8 + cols : 8 + HALO + cols, :] = right_ref[spare : spare + HALO, :]
    tail = mask_vmem.shape[0] - 8 - HALO - cols
    mask_vmem[8 + HALO + cols :, :] = jnp.zeros((tail, R), jnp.float32)
    mask = None
    if masked:
        mask = lambda k: jnp.broadcast_to(mask_vmem[k + 8 : k + 9, :], (16, R))

    def field(f, carry):
        squared = jnp.dot(
            matrix_ref[f], matrix_ref[f], precision=lax.Precision.HIGHEST, preferred_element_type=jnp.float32
        )
        column_ref[pl.ds(pl.multiple_of(f * levels, 8), levels), :] = jnp.broadcast_to(
            squared[:, surface : surface + 1], (levels, R)
        )
        high, low = split_two(squared)
        stacked = jnp.concatenate(
            [jnp.concatenate([high, high], axis=1), jnp.concatenate([low, jnp.zeros_like(low)], axis=1)], axis=0
        )
        read(f).wait()

        @pl.when(f + 1 < fields)
        def _():
            read(f + 1).start()

        def filter_rows(i, slot):
            first = f * levels + i * 16
            spot = pl.multiple_of(i * 16, 16)

            def column(k):
                if k < 0:
                    return left_ref[pl.ds(first * HALO + k + HALO, 16, stride=HALO), :]
                if k >= cols:
                    return right_ref[pl.ds(first * HALO + k - cols, 16, stride=HALO), :]
                return x_vmem[pl.ds(first * cols + k, 16, stride=cols), :]

            def store(k, plane):
                high, low = split_two(plane)
                y_vmem[pl.ds(spot, 16), k * R : (k + 1) * R] = high
                y_vmem[pl.ds(levels + spot, 16), k * R : (k + 1) * R] = low

            filtered_twice(cols, nu, column, mask, op_ref[...], lhs_ref.at[slot], mid_ref.at[slot], store)

        def filter_some(n, carry):
            for slot in range(side):
                filter_rows(n * side + slot, slot)
            return carry

        lax.fori_loop(0, levels // 16 // side, filter_some, 0)

        for pair in range(cols // 2):
            both = jnp.dot(
                stacked,
                y_vmem[: 2 * levels, 2 * pair * R : 2 * (pair + 1) * R],
                preferred_element_type=jnp.float32,
            )
            mixed = both[:levels] + both[levels:]
            for h in range(2):
                out_vmem[pl.ds(f * rows + 2 * pair + h, levels, stride=cols), :] = mixed[:, h * R : (h + 1) * R]
        write(f).start()
        return carry

    lax.fori_loop(0, fields, field, 0)
    for f in range(fields):
        write(f).wait()


def dynamics_kernel(
    sizes, sea_ref, x_ref, left_ref, right_ref, atm_ref, ocean_ref, mask_ref, *rest
):
    atm_cols, sea_cols = sizes

    @pl.when(sea_ref[0] == 0)
    def _():
        dynamics_part(
            FA, LA, atm_cols, LA - 1, SIDE[0], NU_ATMOS, x_ref, left_ref, right_ref, atm_ref, False, mask_ref, *rest
        )

    @pl.when(sea_ref[0] != 0)
    def _():
        dynamics_part(
            FO, LO, sea_cols, 0, SIDE[1], NU_OCEAN, x_ref, left_ref, right_ref, ocean_ref, True, mask_ref, *rest
        )


def dynamics(is_sea, x, left, right, atm_mixing, ocean_mixing, mask, sizes):
    vmem = pl.BlockSpec(memory_space=pltpu.VMEM)
    hbm = pl.BlockSpec(memory_space=pltpu.HBM)
    rows = x.shape[0]
    widest = max(sizes)
    return pl.pallas_call(
        functools.partial(dynamics_kernel, sizes),
        out_shape=[
            jax.ShapeDtypeStruct((rows, R), jnp.float32),
            jax.ShapeDtypeStruct((FA * LA, R), jnp.float32),
            jax.ShapeDtypeStruct((widest + 16, R), jnp.float32),
        ],
        in_specs=[pl.BlockSpec(memory_space=pltpu.SMEM), hbm] + [vmem] * 5,
        out_specs=[hbm, vmem, vmem],
        scratch_shapes=[
            pltpu.VMEM((rows, R), jnp.float32),
            pltpu.VMEM((rows, R), jnp.float32),
            pltpu.VMEM((2 * R, 2 * R), jnp.bfloat16),
            pltpu.VMEM((2 * LA, widest * R), jnp.bfloat16),
            pltpu.VMEM((max(SIDE), 2, (widest + 6) * 16, 2 * R), jnp.bfloat16),
            pltpu.VMEM((max(SIDE), (widest + 4) * 16, R), jnp.float32),
            pltpu.SemaphoreType.DMA((FO,)),
            pltpu.SemaphoreType.DMA((FO,)),
        ],
        compiler_params=pltpu.CompilerParams(vmem_limit_bytes=LIMIT * MIB),
        cost_estimate=pl.CostEstimate(
            flops=100 * rows * R * R, bytes_accessed=16 * rows * R, transcendentals=0
        ),
        name="dynamics",
    )(is_sea, x, left, right, atm_mixing, ocean_mixing, mask)


def lane_edges(rows):
    lane = lax.broadcasted_iota(jnp.int32, (rows, R), 1)
    return lane == 0, lane == R - 1


def lap(before, middle, after, edges):
    first, last = edges
    down = jnp.where(first, 0.0, pltpu.roll(middle, 1, 1))
    up = jnp.where(last, 0.0, pltpu.roll(middle, R - 1, 1))
    return (before + after) + (down + up) - 4.0 * middle


def filter_forcing(f, cols, nu, forcing_of, masked, mask_ref, work_ref, g_ref):
    lo, hi, rows = 8, 8 + cols, cols + 16
    edges = lane_edges(rows)
    mask = mask_ref[0:rows, :]

    def along(v):
        return lap(pltpu.roll(v, 1, 0), v, pltpu.roll(v, rows - 1, 0), edges)

    work_ref[0:rows, :] = jnp.zeros((rows, R), jnp.float32)
    work_ref[lo - HALO : hi + HALO, :] = COUPLE_RATE * forcing_of(f)
    value = work_ref[0:rows, :] * mask
    for _ in range(2):
        value = value - nu * along(along(value))
        if masked:
            value = value * mask
    g_ref[f, :cols] = value[lo:hi]


def update_part(
    cols, levels, fields, pieces, masked, nu, comp_ref, column_ref, part_ref, first_ref, second_ref, mine_ref, mask_ref, out_ref,
    work_ref, g_ref, stage_ref, out_sems
):
    per_piece = fields * levels // pieces
    rows = per_piece * cols

    def write(p):
        span = pl.ds(pl.multiple_of(p * rows, 8), rows)
        return pltpu.make_async_copy(stage_ref.at[span], out_ref.at[span], out_sems.at[p])

    wide = cols + 2 * HALO

    def forcing_of(f):
        if fields == FO:
            return first_ref[0, f, :wide] + second_ref[f, :wide]
        own = first_ref[1, f, :wide] + mine_ref[f, :wide]
        return jnp.where(comp_ref[0] == 2, own, 0.0) + second_ref[f, :wide]

    def piece(p, carry):
        field = p * per_piece // levels

        @pl.when(field < FA)
        def _():
            pushed = [g_ref[field, v * 8 : v * 8 + 8, :] for v in range(cols // 8)]

            def group(q, carry):
                number = p * per_piece + q
                factor = jnp.broadcast_to(column_ref[pl.ds(number, 1), :], (8, R))
                for v in range(cols // 8):
                    span = pl.ds(pl.multiple_of(number * cols + v * 8, 8), 8)
                    stage_ref[span, :] = part_ref[span, :] + factor * pushed[v]
                return carry

            lax.fori_loop(0, per_piece, group, 0, unroll=8)

        @pl.when(field >= FA)
        def _():
            span = pl.ds(pl.multiple_of(p * rows, 8), rows)
            stage_ref[span, :] = part_ref[span, :]

        write(p).start()
        return carry

    per_field = pieces // fields
    for f in range(fields):
        if f < FA:
            filter_forcing(f, cols, nu, forcing_of, masked, mask_ref, work_ref, g_ref)
        lax.fori_loop(f * per_field, (f + 1) * per_field, piece, 0)
    for p in range(pieces):
        write(p).wait()


def fetch_kernel(part_ref, after_ref, out_ref, sems):
    rows = part_ref.shape[0] // 8
    copies = []
    for p in range(8):
        span = pl.ds(p * rows, rows)
        copies.append(pltpu.make_async_copy(part_ref.at[span], out_ref.at[span], sems.at[p]))
        copies[-1].start()
    for copy in copies:
        copy.wait()


def fetch(part, after):
    vmem = pl.BlockSpec(memory_space=pltpu.VMEM)
    hbm = pl.BlockSpec(memory_space=pltpu.HBM)
    return pl.pallas_call(
        fetch_kernel,
        out_shape=pltpu.VMEM(part.shape, jnp.float32),
        in_specs=[hbm, hbm],
        out_specs=vmem,
        scratch_shapes=[pltpu.SemaphoreType.DMA((8,))],
        compiler_params=pltpu.CompilerParams(vmem_limit_bytes=40 * MIB),
        cost_estimate=pl.CostEstimate(flops=0, bytes_accessed=4 * part.size, transcendentals=0),
        name="fetch",
    )(part, after)


def update_kernel(sizes, comp_ref, *rest):
    atm_cols, sea_cols = sizes

    @pl.when(comp_ref[0] != 3)
    def _():
        update_part(atm_cols, LA, FA, 4 * FA, False, NU_ATMOS, comp_ref, *rest)

    @pl.when(comp_ref[0] == 3)
    def _():
        update_part(sea_cols, LO, FO, 2 * FO, True, NU_OCEAN, comp_ref, *rest)


def update(comp, column, part, first, second, mine, mask, sizes):
    vmem = pl.BlockSpec(memory_space=pltpu.VMEM)
    hbm = pl.BlockSpec(memory_space=pltpu.HBM)
    rows = part.shape[0]
    return pl.pallas_call(
        functools.partial(update_kernel, sizes),
        out_shape=jax.ShapeDtypeStruct((rows, R), jnp.float32),
        in_specs=[pl.BlockSpec(memory_space=pltpu.SMEM)] + [vmem] * 6,
        out_specs=hbm,
        scratch_shapes=[
            pltpu.VMEM((max(sizes) + 16, R), jnp.float32),
            pltpu.VMEM((FA, max(sizes), R), jnp.float32),
            pltpu.VMEM((rows, R), jnp.float32),
            pltpu.SemaphoreType.DMA((4 * FA,)),
        ],
        compiler_params=pltpu.CompilerParams(vmem_limit_bytes=40 * MIB),
        cost_estimate=pl.CostEstimate(
            flops=2 * rows * R, bytes_accessed=8 * rows * R, transcendentals=0
        ),
        name="update",
    )(comp, column, part, first, second, mine, mask)


def local(
    fields, atm_mixing, ocean_mixing, sea_mask, source_slot, target_tile, target_slot, remap_blocks
):
    n_comp = lax.axis_size("comp")
    n_tile = lax.axis_size("tile")
    is_sea = lax.axis_index("comp") == n_comp - 1
    sea_cols = sea_mask.shape[2]
    atm_cols = sea_cols * 5 // 6
    sizes = (atm_cols, sea_cols)
    sea_flag = is_sea.astype(jnp.int32).reshape(1)
    mask = sea_mask[0, 0]
    state = fields[0, 0]
    tiles = target_tile[0, 0, :, 0]
    weights = remap_blocks[0, 0]
    forward = [(i, (i + 1) % n_tile) for i in range(n_tile)]
    backward = [(b, a) for a, b in forward]

    low_edge, high_edge = edge_columns(sea_flag, state, mask, sizes)
    low_edge, high_edge, tiles = lax.optimization_barrier((low_edge, high_edge, tiles))
    left = lax.ppermute(high_edge, "tile", forward)
    right = lax.ppermute(low_edge, "tile", backward)

    sent, third = remap(
        sea_flag,
        lax.axis_index("tile").reshape(1),
        source_slot.reshape(1, -1),
        tiles.reshape(1, -1),
        target_slot.reshape(1, -1),
        state.reshape(-1, R),
        weights,
        n_tile,
        sizes,
    )
    comp = lax.axis_index("comp")
    handed = lax.ppermute(third, "comp", [(3, 2)])
    comp_flag = comp.reshape(1)
    sent = join(comp_flag, sent, handed)
    received = lax.all_to_all(sent, "tile", split_axis=0, concat_axis=0, tiled=True)

    x = state.reshape(-1, R)
    flat_left = left.reshape(-1, R)
    flat_right = right.reshape(-1, R)
    part, column, wide_mask = dynamics(sea_flag, x, flat_left, flat_right, atm_mixing, ocean_mixing, mask, sizes)

    received, part = lax.optimization_barrier((received, part))
    first, keep, mine = combine(comp_flag, received, sizes)
    other_core = lax.ppermute(first, "comp", [(0, 1), (1, 0), (2, 3), (3, 2)])
    onward = keep + jnp.where(comp == 3, 0.0, other_core[0])
    other_chip = lax.ppermute(onward, "comp", [(0, 2), (2, 0), (1, 3), (3, 1)])
    part = fetch(part, onward)
    done = update(comp_flag, column, part, other_core, other_chip, mine, wide_mask, sizes)
    return done.reshape(1, 1, -1)


def solution(mesh):
    in_specs = (
        P("comp", "tile", None),
        P(),
        P(),
        P("comp", "tile", None, None),
        P("comp", "tile", None),
        P("comp", "tile", None, None),
        P("comp", "tile", None),
        P("comp", "tile", None, None, None),
    )
    out_specs = P("comp", "tile", None)
    return jax.shard_map(local, mesh=mesh, in_specs=in_specs, out_specs=out_specs, check_vma=False)
```
